32 devices in a mesh: ccd: 4 (over z), patch: 8 (over y, x, core).
Axes of the slice: x: 2, y: 2, z: 4, core: 2. Of those that a mesh axis runs over, the one named last changes fastest.
Arguments:
- pixel_counts: bfloat16 [4, 1024, 4096], P('ccd', 'patch'), may hold values from -1.5 to 14
- pixel_weights: bfloat16 [4, 1024, 4096], P('ccd', 'patch'), may hold values from 0.5 to 2
- wave_profile: bfloat16 [4, 8, 64, 128, 128], P('ccd', 'patch'), may hold values from 0 to 1.65
- cross_profile: bfloat16 [4, 128, 16], P('ccd', 'patch'), may hold values from 0 to 1.5
- trace_columns: int32 [4, 128, 16], P('ccd', 'patch'), may hold values from -8 to 1031, as said below
- throughput: float32 [4], P('ccd'), may hold values from 0.8 to 3.75
- sky_fibres: int32 [4, 16], P('ccd'), may hold values from 0 to 127, as said below
- fibre_mask: int32 [4, 128], P('ccd'), may hold values 0 or 1
Outputs:
- calibrated: float32 [4, 128, 4096], P('ccd', None, 'patch')
- sky_model: float32 [4096], P('patch')
The draws below stay inside these ranges and needn't reach their ends.
Inputs may be any that keep to these rules, and one draw needn't show every extreme that they name: trace_columns[c, f] lists 16 consecutive pixel columns in rising order, numbered from the camera's first column; each lies within 8 columns of the columns 8 * 16 * g to 8 * 16 * (g + 1) - 1 of the fibre's bundle g = f // 16. `sky_fibres`: each row holds 16 different fibre numbers.
All inputs are finite; a program needn't handle non-finite values. No bound on the sum of `fibre_mask` on one device may be relied on, other than what follows from the above.
Results may differ from the reference program's by a relative error of at most 0.0065.
Values may be sent and summed in bfloat16 or wider, within the bound.
No kernel may reach another device: no remote copies, remote signals or barrier semaphores. Data moves between devices by JAX's collectives and lax.ppermute only.
A program may use at most 64 MiB of HBM per device.

```python
import math
import jax
import jax.numpy as jnp
from jax import lax

FIB_DEV = 16
COL_FIB = 8
LW = 64
NWP = 64
ITERS = 10
HALO = 8
KW = 16
WIN = 128
CAMS = 4
FIBRES = 128
COLUMNS = 1024
WAVE = 4096
NSKY = 16
N_PATCH = 8


def sky_choice(key):
    base = jax.random.fold_in(key, 101)
    keys = jax.random.split(base, CAMS)
    orders = jax.vmap(lambda single: jax.random.permutation(single, FIBRES))(keys)
    return orders[:, :NSKY].astype(jnp.int32)


def gain_values(key):
    base = jax.random.fold_in(key, 202)
    camera = jnp.arange(CAMS, dtype=jnp.float32)
    rising = jnp.exp(math.log(3.0) * camera / (CAMS - 1))
    return rising * jax.random.uniform(base, (CAMS,), jnp.float32, 0.8, 1.25)


def draw_throughput(key, part):
    return gain_values(key)


def draw_sky_fibres(key, part):
    return sky_choice(key)


def draw_pixel_counts(key, part):
    chosen = sky_choice(key)
    fibres = jnp.arange(FIBRES, dtype=jnp.int32)
    is_sky = jnp.any(chosen[:, :, None] == fibres[None, None, :], axis=1)
    science = 1.0 - is_sky.astype(jnp.float32)
    gains = gain_values(key)
    key_sky, key_object, key_level, key_noise = jax.random.split(jax.random.fold_in(key, 303), 4)
    sky_row = jax.random.uniform(key_sky, (WAVE,), jnp.float32, 0.3, 1.5)
    object_row = jax.random.uniform(key_object, (WAVE,), jnp.float32, 0.3, 1.5)
    level = jnp.exp(jax.random.uniform(key_level, (CAMS, FIBRES), jnp.float32, 0.0, math.log(4.0)))
    column_fibre = jnp.arange(COLUMNS, dtype=jnp.int32) // COL_FIB
    object_level = jnp.take(science * level, column_fibre, axis=1)
    noise = 0.5 * jnp.clip(jax.random.normal(key_noise, (CAMS, COLUMNS, WAVE), jnp.float32), -3.0, 3.0)
    return (gains[:, None, None] * sky_row[None, None, :] + object_level[:, :, None] * object_row[None, None, :] + noise).astype(jnp.bfloat16)


def draw_trace_columns(key, part):
    fibres = jnp.arange(FIBRES, dtype=jnp.int32)
    jitter = jax.random.randint(jax.random.fold_in(key, 404), (CAMS, FIBRES), -(COL_FIB // 2), COL_FIB // 2 + 1, dtype=jnp.int32)
    start = fibres[None, :] * COL_FIB + COL_FIB // 2 + jitter - COL_FIB
    return (start[:, :, None] + jnp.arange(KW, dtype=jnp.int32)[None, None, :]).astype(jnp.int32)


def draw_cross_profile(key, part):
    offset = jnp.arange(KW, dtype=jnp.float32) - COL_FIB
    spread = 0.45 * COL_FIB
    curve = jnp.exp(-0.5 * (offset / spread) ** 2)
    rough = jax.random.uniform(jax.random.fold_in(key, 505), (CAMS, FIBRES, KW), jnp.float32, 0.5, 1.5)
    return (curve[None, None, :] * rough).astype(jnp.bfloat16)


def draw_wave_profile(key, part):
    rows = jnp.arange(WIN, dtype=jnp.float32)
    offset = rows[:, None] - rows[None, :]
    curve = jnp.exp(-0.5 * offset * offset)
    key_near, key_far = jax.random.split(jax.random.fold_in(key, 606))
    shape = (CAMS, N_PATCH, NWP, WIN, WIN)
    rough = jax.random.uniform(key_near, shape, jnp.float32, 0.5, 1.5)
    floor_level = 0.008
    spread_far = jax.random.uniform(key_far, shape, jnp.float32, 0.0, 2.0)
    return (curve[None, None, None, :, :] * rough + floor_level * spread_far).astype(jnp.bfloat16)


def plant(values, stream_key, low, largest):
    longest = values.shape.index(max(values.shape))
    spots = []
    for shift in (0, 1):
        where = [jax.random.randint(jax.random.fold_in(stream_key, axis), (), 0, length) for axis, length in enumerate(values.shape)]
        where[longest] = (where[longest] + shift) % values.shape[longest]
        spots.append(tuple(where))
    return values.at[spots[0]].set(low).at[spots[1]].set(largest)


def block_levels(stream_key, extent, cuts, low, largest):
    gain = 1.0
    for axis_at, shards_of in cuts:
        steps = jax.random.uniform(jax.random.fold_in(jax.random.fold_in(stream_key, 6), axis_at), (shards_of,), jnp.float32, low / len(cuts), largest / len(cuts))
        gain = gain * jnp.repeat(jnp.exp(steps), extent[axis_at] // shards_of).reshape((-1,) + (1,) * (len(extent) - 1 - axis_at))
    return gain


def setup_inputs(seed: int = 0) -> dict:
    seeds = jax.random.split(jax.random.key(seed), 9)
    return {
        "pixel_counts": draw_pixel_counts(jax.random.fold_in(seeds[8], 71), 0),
        "pixel_weights": jnp.clip(jnp.exp(math.log(2.0) - 1.3862944 * jax.random.uniform(seeds[1], (CAMS, COLUMNS, WAVE), jnp.float32) ** block_levels(seeds[1], (CAMS, COLUMNS, WAVE), ((0, 4), (1, 8)), -0.2, 0.2)), 0.5, 2.0).astype(jnp.bfloat16),
        "wave_profile": draw_wave_profile(jax.random.fold_in(seeds[8], 71), 0),
        "cross_profile": draw_cross_profile(jax.random.fold_in(seeds[8], 71), 0),
        "trace_columns": draw_trace_columns(jax.random.fold_in(seeds[8], 71), 0),
        "throughput": draw_throughput(jax.random.fold_in(seeds[8], 71), 0),
        "sky_fibres": draw_sky_fibres(jax.random.fold_in(seeds[8], 71), 0),
        "fibre_mask": plant((jax.random.randint(seeds[7], (CAMS, FIBRES), 0, 8) < 7).astype(jnp.int32), jax.random.fold_in(seeds[7], 1), 0, 1),
    }


RIDGE = 0.1
PRIOR = 1.0


def round_half(values):
    return lax.optimization_barrier(values.astype(jnp.bfloat16)).astype(jnp.float32)


def make_windows(pixel_block):
    margin = LW // 2
    padded = jnp.pad(pixel_block, ((0, 0), (margin, margin)))
    pieces = padded.reshape(pixel_block.shape[0], NWP + 1, LW)
    return jnp.concatenate([pieces[:, :-1], pieces[:, 1:]], axis=2)


def profile_matrix(local_columns, cross_rows, window_width):
    columns = jnp.arange(window_width, dtype=jnp.int32)
    matches = local_columns[:, :, None] == columns[None, None, :]
    summed = jnp.sum(jnp.where(matches, cross_rows.astype(jnp.float32)[:, :, None], jnp.float32(0.0)), axis=1)
    return summed.T.astype(jnp.bfloat16)


def extract_patches(counts_window, weights_window, profile, wave_rows):
    profile_wide = profile.astype(jnp.float32)
    wave_wide = wave_rows.astype(jnp.float32)
    column_total = jnp.sum(profile_wide, axis=1)
    spread_profile = round_half(profile_wide * column_total[:, None])
    row_total = jnp.sum(wave_wide, axis=2)
    spread_wave = round_half(wave_wide * row_total[:, :, None])
    counts_wide = counts_window.astype(jnp.float32)
    weights_wide = weights_window.astype(jnp.float32)
    mixed_sum = round_half(jnp.einsum('cf,cpr->fpr', spread_profile, weights_wide))
    row_weight = jnp.einsum('fpr,prl->fpl', mixed_sum, spread_wave) + RIDGE
    fluxes = jnp.zeros(row_weight.shape, jnp.float32)
    for iteration in range(ITERS):
        flux_rounded = round_half(fluxes)
        blurred = round_half(jnp.einsum('fpl,prl->fpr', flux_rounded, wave_wide))
        modelled = jnp.einsum('cf,fpr->cpr', profile_wide, blurred)
        residual = round_half(weights_wide * (counts_wide - modelled))
        folded = round_half(jnp.einsum('cf,cpr->fpr', profile_wide, residual))
        gradient = jnp.einsum('fpr,prl->fpl', folded, wave_wide)
        fluxes = fluxes + (gradient - RIDGE * fluxes) / row_weight
    return fluxes, row_weight


def reference(pixel_counts, pixel_weights, wave_profile, cross_profile, trace_columns, throughput, sky_fibres, fibre_mask):
    column_count = FIB_DEV * COL_FIB
    window_width = column_count + 2 * HALO
    counts_padded = jnp.pad(pixel_counts, ((0, 0), (HALO, HALO), (0, 0)))
    weights_padded = jnp.pad(pixel_weights, ((0, 0), (HALO, HALO), (0, 0)))
    zero_index = jnp.zeros((), jnp.int32)
    margin = LW // 2

    def one_bundle(camera_index, bundle_index):
        first_column = (bundle_index * column_count).astype(jnp.int32)
        counts_block = lax.dynamic_slice(counts_padded, (camera_index, first_column, zero_index), (1, window_width, WAVE))[0]
        weights_block = lax.dynamic_slice(weights_padded, (camera_index, first_column, zero_index), (1, window_width, WAVE))[0]
        first_fibre = (bundle_index * FIB_DEV).astype(jnp.int32)
        trace_block = lax.dynamic_slice(trace_columns, (camera_index, first_fibre, zero_index), (1, FIB_DEV, KW))[0]
        cross_block = lax.dynamic_slice(cross_profile, (camera_index, first_fibre, zero_index), (1, FIB_DEV, KW))[0]
        wave_block = lax.dynamic_slice(wave_profile, (camera_index, bundle_index, zero_index, zero_index, zero_index), (1, 1, NWP, WIN, WIN))[0, 0]
        local_columns = (trace_block - (first_column - HALO)).astype(jnp.int32)
        profile = profile_matrix(local_columns, cross_block, window_width)
        fluxes, row_weight = extract_patches(make_windows(counts_block), make_windows(weights_block), profile, wave_block)
        kept = fluxes[:, :, margin:margin + LW].reshape(FIB_DEV, WAVE)
        kept_weight = row_weight[:, :, margin:margin + LW].reshape(FIB_DEV, WAVE)
        return kept, kept_weight

    def one_camera(camera_index):
        bundles = jnp.arange(N_PATCH, dtype=jnp.int32)
        return jax.vmap(lambda bundle_index: one_bundle(camera_index, bundle_index))(bundles)

    extracted, extracted_weight = lax.map(one_camera, jnp.arange(CAMS, dtype=jnp.int32))
    extracted = extracted.reshape(CAMS, FIBRES, WAVE)
    extracted_weight = extracted_weight.reshape(CAMS, FIBRES, WAVE)
    fibres = jnp.arange(FIBRES, dtype=jnp.int32)
    is_sky = jnp.any(sky_fibres[:, :, None] == fibres[None, None, :], axis=1)
    mask_wide = fibre_mask.astype(jnp.float32)
    selected = mask_wide * is_sky.astype(jnp.float32)
    gains = throughput[:, None, None]
    sky_sum = jnp.sum(selected[:, :, None] * gains * extracted_weight * extracted, axis=(0, 1))
    sky_weight = PRIOR + jnp.sum(selected[:, :, None] * gains * gains * extracted_weight, axis=(0, 1))
    sky_model = sky_sum / sky_weight
    calibrated = mask_wide[:, :, None] * (extracted - gains * sky_model[None, None, :])
    return calibrated, sky_model
```

```python
import functools
import jax, jax.numpy as jnp
from jax import lax
from jax.sharding import PartitionSpec as P
from jax.experimental import pallas as pl
from jax.experimental.pallas import tpu as pltpu

LW=64; ITERS=10; HALO=8; RIDGE=0.1; PRIOR=1.0
F32=jnp.float32; BF=jnp.bfloat16
NT=(((1,),(1,)),((),()))

def mm(a,b): return jnp.dot(a,b,preferred_element_type=F32)
def mmt(a,b): return lax.dot_general(a,b,NT,preferred_element_type=F32)

def kernel(group, pc, pw, halo, wave, cols, cross, pick, out, wpad, cpad, qt, A, B0, inv, flux, rw, wt):
    g=pl.program_id(0)
    columns=pc.shape[0]; wavec=pc.shape[1]; rows=columns+2*HALO
    nf=cols.shape[0]
    @pl.when(g==0)
    def _():
        for pad,src,i in ((cpad,pc,0),(wpad,pw,1)):
            z=jnp.zeros((rows,128),BF)
            pad[:,:128]=z
            pad[:,wavec+128:]=z
            pad[:columns,128:wavec+128]=src[...]
            pad[columns:,128:wavec+128]=halo[i]
        j=lax.broadcasted_iota(jnp.int32,(nf,rows),1)
        col=jnp.where(j<columns,j,jnp.where(j<columns+HALO,j-columns-HALO,j-HALO))
        pt=jnp.zeros((nf,rows),F32)
        for k in range(cols.shape[1]):
            pt=pt+jnp.where(cols[:,k:k+1]==col,cross[:,k:k+1].astype(F32),0.0)
        pt=pt.astype(BF).astype(F32)
        tot=jnp.sum(pt,axis=0,keepdims=True)
        for f in range(nf):
            q=pt*pt[f:f+1,:]
            hi=q.astype(BF)
            qt[f*nf:(f+1)*nf,:]=hi
            qt[(nf+f)*nf:(nf+f+1)*nf,:]=(q-hi.astype(F32)).astype(BF)
        n2=2*nf*nf
        qt[n2:n2+nf,:]=(pt*tot).astype(BF)
        qt[n2+nf:n2+2*nf,:]=pt.astype(BF)
    n1=nf*nf; n2=2*nf*nf
    z=jnp.zeros((nf,128),BF)
    def pairmm(a,b,m):
        a=a.astype(BF); b=b.astype(BF)
        l=jnp.concatenate([jnp.concatenate([a,z],axis=1),jnp.concatenate([z,b],axis=1)],axis=0)
        r=mm(l,m)
        return r[:nf],r[nf:]
    def two(ref,k):
        return ref[2*k:2*k+2].reshape(256,128) if isinstance(k,int) else ref[pl.ds(2*k,2)].reshape(256,128)
    def build(k,_):
        base=pl.multiple_of(g*(group*LW)+k*128,128)
        w3=wpad[:,pl.ds(base,384)].astype(F32)
        c3=cpad[:,pl.ds(base,384)].astype(F32)
        def win(v):
            return jnp.concatenate([v[:,96:224],v[:,160:288]],axis=1)
        w=win(w3)
        wc=w*win(c3)
        wb=w.astype(BF)
        hi=wc.astype(BF)
        lo=(wc-hi.astype(F32)).astype(BF)
        a=mm(qt[:n2+nf,:],wb)
        aa=a[:n1]+a[n1:n2]
        mixed=a[n2:].astype(BF).astype(F32)
        ptb=qt[n2+nf:,:]
        b=mm(ptb,hi)+mm(ptb,lo)
        mr=[]
        for h in range(2):
            p=2*k+h
            t=wave[p].T
            wt[p]=t
            rt=jnp.sum(t.astype(F32),axis=0,keepdims=True)
            mr.append(mixed[:,128*h:128*h+128]*rt)
            A[p]=aa[:,128*h:128*h+128]
            B0[p]=b[:,128*h:128*h+128]
        wv=two(wave,k)
        r=pairmm(*mr,wv)
        fl=pairmm(b[:,:128],b[:,128:],wv)
        for h in range(2):
            p=2*k+h
            rh=r[h]+RIDGE
            rw[p]=rh
            iv=1.0/rh
            inv[p]=iv
            flux[p]=fl[h]*iv
        return 0
    lax.fori_loop(0,group//2,build,0)
    def sweep(it,_):
        for k in range(group//2):
            fl=[flux[2*k],flux[2*k+1]]
            bl=pairmm(*fl,two(wt,k))
            fo=[]
            for h in range(2):
                p=2*k+h
                acc=B0[p]
                for f in range(nf):
                    acc=acc-A[p,f*nf:(f+1)*nf,:]*bl[h][f:f+1,:]
                fo.append(acc)
            gr=pairmm(*fo,two(wave,k))
            for h in range(2):
                p=2*k+h
                flux[p]=fl[h]+(gr[h]-RIDGE*fl[h])*inv[p]
        return 0
    lax.fori_loop(1,ITERS,sweep,0)
    m=LW//2
    s1=pick[:,0:1]; s2=pick[:,1:2]
    for k in range(group//2):
        fl=jnp.concatenate([flux[2*k,:,m:m+LW],flux[2*k+1,:,m:m+LW]],axis=1)
        rr=jnp.concatenate([rw[2*k,:,m:m+LW],rw[2*k+1,:,m:m+LW]],axis=1)
        sky=jnp.sum(s1*rr*fl,axis=0,keepdims=True)
        wt=jnp.sum(s2*rr,axis=0,keepdims=True)
        per=out.shape[2]//128
        at=slice(128*(k%per),128*(k%per)+128)
        out[k//per,:nf,at]=fl
        out[k//per,nf:,at]=jnp.concatenate([sky,wt,jnp.zeros((6,128),F32)],axis=0)

def extract(pc,pw,halo,wave,cols,cross,pick,parts):
    columns,wavec=pc.shape
    nf=cols.shape[0]; np_=wave.shape[0]; win=wave.shape[1]; group=np_
    rows=columns+2*HALO
    full=lambda shape: pl.BlockSpec(shape,lambda g:(0,)*len(shape))
    shape=(parts,nf+8,wavec//parts)
    return pl.pallas_call(
        functools.partial(kernel,group),
        grid=(1,),
        in_specs=[full(a.shape) for a in (pc,pw,halo,wave,cols,cross,pick)],
        out_specs=full(shape),
        out_shape=jax.ShapeDtypeStruct(shape,F32),
        scratch_shapes=[pltpu.VMEM((rows,wavec+256),BF),pltpu.VMEM((rows,wavec+256),BF),pltpu.VMEM((2*nf*nf+2*nf,rows),BF),
            pltpu.VMEM((group,nf*nf,win),F32)]+[pltpu.VMEM((group,nf,win),F32)]*4+[pltpu.VMEM((group,win,win),BF)],
        compiler_params=pltpu.CompilerParams(vmem_limit_bytes=48*2**20),
    )(pc,pw,halo,wave,cols,cross,pick)


def tree(terms):
    return terms[0] if len(terms)==1 else tree(terms[0::2])+tree(terms[1::2])


def per_device(pixel_counts,pixel_weights,wave_profile,cross_profile,trace_columns,throughput,sky_fibres,fibre_mask):
    columns=pixel_counts.shape[1]; wavec=pixel_counts.shape[2]; nf=trace_columns.shape[1]
    n=lax.axis_size("patch"); nc=lax.axis_size("ccd")
    me=lax.axis_index("patch")
    head=jnp.stack([pixel_counts[0,:HALO],pixel_weights[0,:HALO]])
    tail=jnp.stack([pixel_counts[0,columns-HALO:],pixel_weights[0,columns-HALO:]])
    lo=lax.ppermute(tail,"patch",[(i,i+1) for i in range(n-1)])
    hi=lax.ppermute(head,"patch",[(i+1,i) for i in range(n-1)])
    halo=jnp.concatenate([lo,hi],axis=1)
    gain=throughput[0]
    mask=fibre_mask[0].astype(F32)
    fibres=me*nf+jnp.arange(nf,dtype=jnp.int32)
    sky=jnp.any(sky_fibres[0][None,:]==fibres[:,None],axis=1)
    own=jnp.where(sky,lax.dynamic_slice(mask,(me*nf,),(nf,)),0.0)
    pick=jnp.stack([own*gain,own*(gain*gain)],axis=1)
    out=extract(pixel_counts[0],pixel_weights[0],halo,wave_profile[0,0],trace_columns[0]-me*columns,cross_profile[0],pick,n)
    got=lax.all_to_all(out,"patch",split_axis=0,concat_axis=0,tiled=True)
    part=jnp.sum(got[:,nf:nf+2],axis=0)
    total=tree([part]+[lax.ppermute(part,"ccd",[(i,(i+s)%nc) for i in range(nc)]) for s in range(1,nc)])
    model=total[0]/(PRIOR+total[1])
    flux=got[:,:nf].reshape(n*nf,wavec//n)
    calibrated=mask[:,None]*(flux-gain*model[None,:])
    return calibrated[None],model


def solution(mesh):
    return jax.shard_map(per_device,mesh=mesh,
        in_specs=(P("ccd","patch",None),P("ccd","patch",None),P("ccd","patch",None,None,None),P("ccd","patch",None),P("ccd","patch",None),P("ccd"),P("ccd",None),P("ccd",None)),
        out_specs=(P("ccd",None,"patch"),P("patch")),check_vma=False)
```

```python
import functools
import jax
import jax.numpy as jnp
from jax import lax
from jax.sharding import PartitionSpec as P
from jax.experimental import pallas as pl
from jax.experimental.pallas import tpu as pltpu

LW = 64
ITERS = 10
HALO = 8
RIDGE = 0.1
PRIOR = 1.0
LANES = 128
EXTRA = 8
CHUNKS = 4
F32 = jnp.float32
BF16 = jnp.bfloat16


def mm(a, b):
    return jnp.dot(a, b, preferred_element_type=F32)


def pair_mm(a, b, stacked):
    a = a.astype(BF16)
    b = b.astype(BF16)
    zero = jnp.zeros_like(a)
    left = jnp.concatenate(
        [jnp.concatenate([a, zero], axis=1), jnp.concatenate([zero, b], axis=1)], axis=0
    )
    both = mm(left, stacked)
    return both[: a.shape[0]], both[a.shape[0] :]


def profile_rows(cols, cross, columns):
    fibres = cols.shape[0]
    lane = lax.broadcasted_iota(jnp.int32, (fibres, columns + 2 * HALO), 1)
    column = jnp.where(
        lane < columns, lane, jnp.where(lane < columns + HALO, lane - columns - HALO, lane - HALO)
    )
    total = jnp.zeros(column.shape, F32)
    for k in range(cols.shape[1]):
        total = total + jnp.where(cols[:, k : k + 1] == column, cross[:, k : k + 1].astype(F32), 0.0)
    return total.astype(BF16).astype(F32)


def split(values):
    top = values.astype(BF16)
    return top, (values - top.astype(F32)).astype(BF16)


def prepare_kernel(
    gain, counts, weights, wave, traces, cross, sky, mask,
    terms, first, mixed, turned, row_total, wave_out, side, side_sum, pick, mask_out, gain_out,
    cpad, wpad, main, main_sum, gain_v, traces_v, cross_v, sky_v, mask_v, small, pixel_sem, wave_sem,
):
    me = lax.axis_index("patch")
    columns, wave_count = counts.shape
    fibres = traces.shape[0]
    patches = wave.shape[0]
    square = fibres * fibres

    copies = [
        pltpu.make_async_copy(a, b, small.at[i])
        for i, (a, b) in enumerate(
            ((gain, gain_v), (traces, traces_v), (cross, cross_v), (sky, sky_v), (mask, mask_v))
        )
    ]
    step = wave_count // CHUNKS
    pixel_copies = []
    for c in range(CHUNKS):
        source = pl.ds(c * step, step)
        target = pl.ds(LANES + c * step, step)
        pixel_copies.append(
            [
                pltpu.make_async_copy(counts.at[:, source], cpad.at[:, target], pixel_sem.at[0, c]),
                pltpu.make_async_copy(weights.at[:, source], wpad.at[:, target], pixel_sem.at[1, c]),
            ]
        )
    wave_copy = pltpu.make_async_copy(wave, wave_out, wave_sem)
    for copy in copies:
        copy.start()
    for pair in pixel_copies:
        for copy in pair:
            copy.start()
    wave_copy.start()
    zero = jnp.zeros((columns, LANES), BF16)
    for pad in (cpad, wpad):
        pad[:, :LANES] = zero
        pad[:, LANES + wave_count :] = zero
    for copy in copies:
        copy.wait()

    profile = profile_rows(traces_v[...] - me * columns, cross_v[...], columns)
    spread = (profile * jnp.sum(profile, axis=0, keepdims=True)).astype(BF16)
    for f in range(fibres):
        at = slice(f * fibres, (f + 1) * fibres)
        top, low = split(profile * profile[f : f + 1, :])
        main[at, :] = jnp.concatenate([top[:, :columns], low[:, :columns]], axis=1)
        side[at, :] = jnp.concatenate([top[:, columns:], low[:, columns:]], axis=1)
    half = profile.astype(BF16)
    main[square:, :] = jnp.concatenate([spread[:, :columns], jnp.zeros((fibres, columns), BF16)], axis=1)
    side[square:, :] = jnp.concatenate([spread[:, columns:], jnp.zeros((fibres, 2 * HALO), BF16)], axis=1)
    main_sum[...] = jnp.concatenate([half[:, :columns]] * 2, axis=1)
    side_sum[...] = jnp.concatenate([half[:, columns:]] * 2, axis=1)

    number = me * fibres + lax.broadcasted_iota(jnp.int32, (fibres, sky_v.shape[1]), 0)
    is_sky = jnp.max(jnp.where(number == sky_v[...], 1.0, 0.0), axis=1, keepdims=True)
    count = mask_v.shape[1]
    for b in range(count // fibres):
        row = b * fibres + lax.broadcasted_iota(jnp.int32, (fibres, count), 0)
        lane = lax.broadcasted_iota(jnp.int32, (fibres, count), 1)
        column = jnp.sum(jnp.where(row == lane, mask_v[...].astype(F32), 0.0), axis=1, keepdims=True)
        mask_out[b * fibres : (b + 1) * fibres, :] = jnp.broadcast_to(column, (fibres, LANES))
    scale = gain_v[...]
    own = mask_out[pl.ds(pl.multiple_of(me * fibres, fibres), fibres), :]
    chosen = is_sky * own * scale
    pick[0] = chosen
    pick[1] = chosen * scale
    gain_out[...] = jnp.broadcast_to(scale, gain_out.shape)

    ready = 0
    for k in range(patches // 2):
        need = min(CHUNKS, ((k + 1) * LANES + LW // 2 - 1) // step + 1)
        while ready < need:
            for copy in pixel_copies[ready]:
                copy.wait()
            ready += 1
        start = LANES - LW // 2 + k * LANES

        def window(pad):
            return jnp.concatenate(
                [pad[:, start : start + LANES], pad[:, start + LW : start + LW + LANES]], axis=1
            )

        weight = window(wpad)
        top, low = split(weight.astype(F32) * window(cpad).astype(F32))
        both = mm(main[...], jnp.concatenate([weight, weight], axis=0))
        sums = mm(main_sum[...], jnp.concatenate([top, low], axis=0))
        for h in range(2):
            at = slice(h * LANES, (h + 1) * LANES)
            terms[2 * k + h] = both[:square, at]
            mixed[2 * k + h] = both[square:, at]
            first[2 * k + h] = sums[:, at]

    wave_copy.wait()
    for p in range(patches):
        flipped = wave_out[p].T
        turned[p] = flipped
        total = jnp.sum(flipped.astype(F32), axis=0, keepdims=True)
        row_total[p] = jnp.broadcast_to(total, row_total.shape[1:])


def prepare(gain, counts, weights, wave, traces, cross, sky, mask):
    columns, wave_count = counts.shape
    fibres = traces.shape[0]
    patches, window, _ = wave.shape
    square = fibres * fibres
    far = pl.BlockSpec(memory_space=pltpu.HBM)
    near = pl.BlockSpec(memory_space=pltpu.VMEM)
    shape = jax.ShapeDtypeStruct
    return pl.pallas_call(
        prepare_kernel,
        in_specs=[far] * 8,
        out_specs=[near] * 11,
        out_shape=[
            shape((patches, square, window), F32),
            shape((patches, fibres, window), F32),
            shape((patches, fibres, window), F32),
            shape(wave.shape, BF16),
            shape((patches, 8, window), F32),
            shape(wave.shape, BF16),
            shape((square + fibres, 4 * HALO), BF16),
            shape((fibres, 4 * HALO), BF16),
            shape((2, fibres, LANES), F32),
            shape((mask.shape[1], LANES), F32),
            shape((8, LANES), F32),
        ],
        scratch_shapes=[
            pltpu.VMEM((columns, wave_count + 2 * LANES), BF16),
            pltpu.VMEM((columns, wave_count + 2 * LANES), BF16),
            pltpu.VMEM((square + fibres, 2 * columns), BF16),
            pltpu.VMEM((fibres, 2 * columns), BF16),
            pltpu.VMEM(gain.shape, F32),
            pltpu.VMEM(traces.shape, jnp.int32),
            pltpu.VMEM(cross.shape, BF16),
            pltpu.VMEM(sky.shape, jnp.int32),
            pltpu.VMEM(mask.shape, jnp.int32),
            pltpu.SemaphoreType.DMA((5,)),
            pltpu.SemaphoreType.DMA((2, CHUNKS)),
            pltpu.SemaphoreType.DMA,
        ],
        compiler_params=pltpu.CompilerParams(vmem_limit_bytes=24 * 2**20),
        name="prepare",
    )(gain, counts, weights, wave, traces, cross, sky, mask)


def relax_kernel(
    groups, low, high, terms_own, first_own, mixed_own, turned, row_total, wave, side, side_sum, pick, *rest
):
    outs = rest[: len(groups)]
    wpad, cpad, terms, first, inverse, flux, row_weight = rest[len(groups) :]
    me = lax.axis_index("patch")
    wave_count = low.shape[1]
    square, fibres = terms.shape[1], first.shape[1]
    width = outs[0].shape[-1]
    tiles = width // LANES
    per = width // LW
    flat = [(o, i, s) for o, group in enumerate(groups) for i, s in enumerate(group)]
    owner = [me ^ s for _, _, s in flat]
    pairs = [(g, j) for g in range(len(flat)) for j in range(per // 2)]

    last = wave_count // LANES - 1
    for g in range(len(flat)):
        for t in range(tiles + 2):
            tile = owner[g] * tiles + (t - 1)
            lanes = pl.ds(pl.multiple_of(jnp.clip(tile, 0, last) * LANES, LANES), LANES)
            below = low[:, lanes].astype(F32)
            above = high[:, lanes].astype(F32)
            for i, pad in ((0, cpad), (1, wpad)):
                at = slice(i * HALO, (i + 1) * HALO)
                both = jnp.concatenate([below[at], above[at]], axis=0).astype(BF16)
                if t == 0 or t == tiles + 1:
                    inside = jnp.logical_and(tile >= 0, tile <= last)
                    both = jnp.where(inside, both, jnp.zeros_like(both))
                pad[g, :, t * LANES : (t + 1) * LANES] = both

    for q, (g, j) in enumerate(pairs):
        start = LANES - LW // 2 + j * LANES

        def window(pad):
            return jnp.concatenate(
                [pad[g, :, start : start + LANES], pad[g, :, start + LW : start + LW + LANES]], axis=1
            )

        weight = window(wpad)
        top, bottom = split(weight.astype(F32) * window(cpad).astype(F32))
        both = mm(side[...], jnp.concatenate([weight, weight], axis=0))
        sums = mm(side_sum[...], jnp.concatenate([top, bottom], axis=0))
        for h in range(2):
            p = owner[g] * per + 2 * j + h
            at = slice(h * LANES, (h + 1) * LANES)
            terms[2 * q + h] = terms_own[p] + both[:square, at]
            first[2 * q + h] = first_own[p] + sums[:, at]
            whole_sum = (mixed_own[p] + both[square:, at]).astype(BF16).astype(F32)
            flux[2 * q + h] = whole_sum * row_total[p, 0:1, :]

    def stacked(ref, g, j):
        return ref[pl.ds(owner[g] * per + 2 * j, 2)].reshape(2 * LANES, LANES)

    for q, (g, j) in enumerate(pairs):
        grid = stacked(wave, g, j)
        weight_pair = pair_mm(flux[2 * q], flux[2 * q + 1], grid)
        step_pair = pair_mm(first[2 * q], first[2 * q + 1], grid)
        for h in range(2):
            total = weight_pair[h] + RIDGE
            row_weight[2 * q + h] = total
            reciprocal = 1.0 / total
            inverse[2 * q + h] = reciprocal
            flux[2 * q + h] = step_pair[h] * reciprocal

    def sweep(_, carry):
        for q, (g, j) in enumerate(pairs):
            now = [flux[2 * q], flux[2 * q + 1]]
            blurred = pair_mm(*now, stacked(turned, g, j))
            folded = []
            for h in range(2):
                total = first[2 * q + h]
                for f in range(fibres):
                    term = terms[2 * q + h, f * fibres : (f + 1) * fibres, :]
                    total = total - term * blurred[h][f : f + 1, :]
                folded.append(total)
            gradient = pair_mm(*folded, stacked(wave, g, j))
            for h in range(2):
                flux[2 * q + h] = now[h] + (gradient[h] - RIDGE * now[h]) * inverse[2 * q + h]
        return carry

    lax.fori_loop(1, ITERS, sweep, 0)

    margin = LW // 2
    for q, (g, j) in enumerate(pairs):
        half = slice(j * LANES, (j + 1) * LANES)

        def kept(values):
            return jnp.concatenate(
                [values[2 * q, :, margin : margin + LW], values[2 * q + 1, :, margin : margin + LW]],
                axis=1,
            )

        spectrum = kept(flux)
        strength = kept(row_weight)
        o, i, _ = flat[g]
        outs[o][i, :fibres, half] = spectrum
        outs[o][i, fibres:, half] = jnp.concatenate(
            [
                jnp.sum(pick[0] * strength * spectrum, axis=0, keepdims=True),
                jnp.sum(pick[1] * strength, axis=0, keepdims=True),
                jnp.zeros((EXTRA - 2, LANES), F32),
            ],
            axis=0,
        )


def relax(groups, width, low, high, terms, first, *rest):
    square, window = terms.shape[1:]
    fibres = first.shape[1]
    number = sum(len(group) for group in groups)
    count = number * width // LW
    near = pl.BlockSpec(memory_space=pltpu.VMEM)
    return pl.pallas_call(
        functools.partial(relax_kernel, groups),
        in_specs=[near] * (4 + len(rest)),
        out_specs=[near] * len(groups),
        out_shape=[jax.ShapeDtypeStruct((len(group), fibres + EXTRA, width), F32) for group in groups],
        scratch_shapes=[pltpu.VMEM((number, 2 * HALO, width + 2 * LANES), BF16)] * 2
        + [pltpu.VMEM((count, square, window), F32)]
        + [pltpu.VMEM((count, fibres, window), F32)] * 4,
        compiler_params=pltpu.CompilerParams(vmem_limit_bytes=24 * 2**20),
        name="relax",
    )(low, high, terms, first, *rest)


def finish_kernel(fibres, gain, mask, own, swapped, totals, *rest):
    *across, calibrated, model = rest
    me = lax.axis_index("patch")
    width = model.shape[1]
    sky = totals[0:1, :] / (PRIOR + totals[1:2, :])
    model[...] = sky
    blocks = {0: own[0, :fibres, :], 1: swapped[0, :fibres, :]}
    for t, block in enumerate(across):
        blocks[2 * t + 2] = block[0, :fibres, :]
        blocks[2 * t + 3] = swapped[t + 1, :fibres, :]
    for s, block in blocks.items():
        at = pl.ds(pl.multiple_of((me ^ s) * fibres, fibres), fibres)
        calibrated[at, :] = mask[at, 0:1] * (block - gain[0:1, 0:1] * sky)


def finish(fibres, gain, mask, own, swapped, totals, across):
    width = totals.shape[1]
    near = pl.BlockSpec(memory_space=pltpu.VMEM)
    return pl.pallas_call(
        functools.partial(finish_kernel, fibres),
        in_specs=[near] * (5 + len(across)),
        out_specs=[near] * 2,
        out_shape=[
            jax.ShapeDtypeStruct((mask.shape[0], width), F32),
            jax.ShapeDtypeStruct((1, width), F32),
        ],
        name="finish",
    )(gain, mask, own, swapped, totals, *across)


def tree(terms):
    return terms[0] if len(terms) == 1 else tree(terms[0::2]) + tree(terms[1::2])


def swap(values, axis, shift):
    return lax.ppermute(values, axis, [(i, i ^ shift) for i in range(lax.axis_size(axis))])


def edges(counts, weights):
    columns = counts.shape[0]
    parts = lax.axis_size("patch")
    me = lax.axis_index("patch")
    odd = me % 2 == 1
    first = jnp.concatenate([counts[:HALO], weights[:HALO]], axis=0)
    final = jnp.concatenate([counts[columns - HALO :], weights[columns - HALO :]], axis=0)
    far = [(i, i + 1) for i in range(1, parts - 1, 2)]
    outer = lax.ppermute(jnp.where(odd, final, first), "patch", far + [(b, a) for a, b in far])
    inner = swap(jnp.where(odd, first, final), "patch", 1)
    return jnp.where(odd, inner, outer), jnp.where(odd, outer, inner)


def per_device(
    pixel_counts,
    pixel_weights,
    wave_profile,
    cross_profile,
    trace_columns,
    throughput,
    sky_fibres,
    fibre_mask,
):
    fibres = trace_columns.shape[1]
    parts = lax.axis_size("patch")
    cameras = lax.axis_size("ccd")
    width = pixel_counts.shape[2] // parts
    low, high = edges(pixel_counts[0], pixel_weights[0])
    *state, mask, gain = prepare(
        throughput[None, :],
        pixel_counts[0],
        pixel_weights[0],
        wave_profile[0, 0],
        trace_columns[0],
        cross_profile[0],
        sky_fibres,
        fibre_mask,
    )
    away = relax([(s, s + 1) for s in range(2, parts, 2)], width, low, high, *state)
    across = [swap(block, "patch", 2 * t + 2) for t, block in enumerate(away)]
    state[0], *away = lax.optimization_barrier((state[0], *away))
    own, mate = relax([(0,), (1,)], width, low, high, *state)
    swapped = swap(jnp.concatenate([mate] + [block[1:] for block in across], axis=0), "patch", 1)
    sky = slice(fibres, fibres + 2)
    part = own[0, sky] + jnp.sum(swapped[:, sky], axis=0)
    for block in across:
        part = part + block[0, sky]
    totals = tree([part] + [swap(part, "ccd", s) for s in range(1, cameras)])
    calibrated, model = finish(fibres, gain, mask, own, swapped, totals, across)
    return calibrated[None], model[0]


def solution(mesh):
    return jax.shard_map(
        per_device,
        mesh=mesh,
        in_specs=(
            P("ccd", "patch", None),
            P("ccd", "patch", None),
            P("ccd", "patch", None, None, None),
            P("ccd", "patch", None),
            P("ccd", "patch", None),
            P("ccd"),
            P("ccd", None),
            P("ccd", None),
        ),
        out_specs=(P("ccd", None, "patch"), P("patch")),
        check_vma=False,
    )
```

```python
import functools
import jax
import jax.numpy as jnp
from jax import lax
from jax.sharding import PartitionSpec as P
from jax.experimental import pallas as pl
from jax.experimental.pallas import tpu as pltpu

LW = 64
ITERS = 10
HALO = 8
RIDGE = 0.1
PRIOR = 1.0
LANES = 128
EXTRA = 8
F32 = jnp.float32
BF16 = jnp.bfloat16


def mm(a, b):
    return jnp.dot(a, b, preferred_element_type=F32)


def pair_mm(a, b, stacked):
    a = a.astype(BF16)
    b = b.astype(BF16)
    zero = jnp.zeros_like(a)
    left = jnp.concatenate(
        [jnp.concatenate([a, zero], axis=1), jnp.concatenate([zero, b], axis=1)], axis=0
    )
    both = mm(left, stacked)
    return both[: a.shape[0]], both[a.shape[0] :]


def profile_rows(cols, cross, columns):
    fibres = cols.shape[0]
    lane = lax.broadcasted_iota(jnp.int32, (fibres, columns + 2 * HALO), 1)
    column = jnp.where(
        lane < columns, lane, jnp.where(lane < columns + HALO, lane - columns - HALO, lane - HALO)
    ).astype(F32)
    total = jnp.zeros(column.shape, F32)
    for k in range(cols.shape[1]):
        total = total + jnp.where(cols[:, k : k + 1] == column, cross[:, k : k + 1], 0.0)
    return total.astype(BF16).astype(F32)


def split(values):
    top = values.astype(BF16)
    return top, (values - top.astype(F32)).astype(BF16)


def prepare_kernel(
    small, pixels, wave,
    terms, first, mixed, turned, row_total, side, side_sum, main, main_sum,
):
    columns = pixels.shape[0] // 2
    fibres = first.shape[1]
    patches = wave.shape[0]
    square = fibres * fibres
    taps = 2 * HALO

    profile = profile_rows(small[:fibres, :taps], small[:fibres, taps : 2 * taps], columns)
    spread = (profile * jnp.sum(profile, axis=0, keepdims=True)).astype(BF16)
    for f in range(fibres):
        at = slice(f * fibres, (f + 1) * fibres)
        top, low = split(profile * profile[f : f + 1, :])
        main[at, :] = jnp.concatenate([top[:, :columns], low[:, :columns]], axis=1)
        side[at, :] = jnp.concatenate([top[:, columns:], low[:, columns:]], axis=1)
    half = profile.astype(BF16)
    main[square:, :] = jnp.concatenate([spread[:, :columns], jnp.zeros((fibres, columns), BF16)], axis=1)
    side[square:, :] = jnp.concatenate([spread[:, columns:], jnp.zeros((fibres, 2 * HALO), BF16)], axis=1)
    main_sum[...] = jnp.concatenate([half[:, :columns]] * 2, axis=1)
    side_sum[...] = jnp.concatenate([half[:, columns:]] * 2, axis=1)

    for k in range(patches // 2):
        start = LANES - LW // 2 + k * LANES

        def window(rows):
            return jnp.concatenate(
                [pixels[rows, start : start + LANES], pixels[rows, start + LW : start + LW + LANES]], axis=1
            )

        weight = window(slice(columns, 2 * columns))
        top, low = split(weight.astype(F32) * window(slice(columns)).astype(F32))
        both = mm(main[...], jnp.concatenate([weight, weight], axis=0))
        sums = mm(main_sum[...], jnp.concatenate([top, low], axis=0))
        for h in range(2):
            at = slice(h * LANES, (h + 1) * LANES)
            terms[2 * k + h] = both[:square, at]
            mixed[2 * k + h] = both[square:, at]
            first[2 * k + h] = sums[:, at]

    for p in range(patches):
        flipped = wave[p].T
        turned[p] = flipped
        total = jnp.sum(flipped.astype(F32), axis=0, keepdims=True)
        row_total[p] = jnp.broadcast_to(total, row_total.shape[1:])


def prepare(small, pixels, wave, fibres):
    columns = pixels.shape[0] // 2
    patches, window, _ = wave.shape
    square = fibres * fibres
    near = pl.BlockSpec(memory_space=pltpu.VMEM)
    shape = jax.ShapeDtypeStruct
    return pl.pallas_call(
        prepare_kernel,
        in_specs=[near] * 3,
        out_specs=[near] * 7,
        out_shape=[
            shape((patches, square, window), F32),
            shape((patches, fibres, window), F32),
            shape((patches, fibres, window), F32),
            shape(wave.shape, BF16),
            shape((patches, 8, window), F32),
            shape((square + fibres, 4 * HALO), BF16),
            shape((fibres, 4 * HALO), BF16),
        ],
        scratch_shapes=[
            pltpu.VMEM((square + fibres, 2 * columns), BF16),
            pltpu.VMEM((fibres, 2 * columns), BF16),
        ],
        compiler_params=pltpu.CompilerParams(vmem_limit_bytes=8 * 2**20),
        name="prepare",
    )(small, pixels, wave)


def relax_kernel(
    groups, outer, inner, terms_own, first_own, mixed_own, turned, row_total, side, side_sum, small, wave, *rest
):
    outs = rest[: len(groups)]
    mask_out, gain_out, wpad, cpad, terms, first, inverse, flux, row_weight = rest[len(groups) :]
    me = lax.axis_index("patch")
    odd = me % 2 == 1
    square, fibres = terms.shape[1], first.shape[1]
    width = outs[0].shape[-1]
    tiles = width // LANES
    per = width // LW
    flat = [(o, i, s) for o, group in enumerate(groups) for i, s in enumerate(group)]
    owner = [me ^ s for _, _, s in flat]
    pairs = [(g, j) for g in range(len(flat)) for j in range(per // 2)]

    for g in range(len(flat)):
        for t in range(tiles + 2):
            lanes = pl.ds(pl.multiple_of((owner[g] * tiles + t) * LANES, LANES), LANES)
            near = inner[:, lanes].astype(F32)
            far = outer[:, lanes].astype(F32)
            below = jnp.where(odd, near, far)
            above = jnp.where(odd, far, near)
            for i, pad in ((0, cpad), (1, wpad)):
                at = slice(i * HALO, (i + 1) * HALO)
                both = jnp.concatenate([below[at], above[at]], axis=0).astype(BF16)
                pad[g, :, t * LANES : (t + 1) * LANES] = both

    for q, (g, j) in enumerate(pairs):
        start = LANES - LW // 2 + j * LANES

        def window(pad):
            return jnp.concatenate(
                [pad[g, :, start : start + LANES], pad[g, :, start + LW : start + LW + LANES]], axis=1
            )

        weight = window(wpad)
        top, bottom = split(weight.astype(F32) * window(cpad).astype(F32))
        both = mm(side[...], jnp.concatenate([weight, weight], axis=0))
        sums = mm(side_sum[...], jnp.concatenate([top, bottom], axis=0))
        for h in range(2):
            p = owner[g] * per + 2 * j + h
            at = slice(h * LANES, (h + 1) * LANES)
            terms[2 * q + h] = terms_own[p] + both[:square, at]
            first[2 * q + h] = first_own[p] + sums[:, at]
            whole_sum = (mixed_own[p] + both[square:, at]).astype(BF16).astype(F32)
            flux[2 * q + h] = whole_sum * row_total[p, 0:1, :]

    def stacked(ref, g, j):
        return ref[pl.ds(owner[g] * per + 2 * j, 2)].reshape(2 * LANES, LANES)

    for q, (g, j) in enumerate(pairs):
        grid = stacked(wave, g, j)
        weight_pair = pair_mm(flux[2 * q], flux[2 * q + 1], grid)
        step_pair = pair_mm(first[2 * q], first[2 * q + 1], grid)
        for h in range(2):
            total = weight_pair[h] + RIDGE
            row_weight[2 * q + h] = total
            reciprocal = 1.0 / total
            inverse[2 * q + h] = reciprocal
            flux[2 * q + h] = step_pair[h] * reciprocal

    def sweep(_, carry):
        for q, (g, j) in enumerate(pairs):
            now = [flux[2 * q], flux[2 * q + 1]]
            blurred = pair_mm(*now, stacked(turned, g, j))
            folded = []
            for h in range(2):
                total = first[2 * q + h]
                for f in range(fibres):
                    term = terms[2 * q + h, f * fibres : (f + 1) * fibres, :]
                    total = total - term * blurred[h][f : f + 1, :]
                folded.append(total)
            gradient = pair_mm(*folded, stacked(wave, g, j))
            for h in range(2):
                flux[2 * q + h] = now[h] + (gradient[h] - RIDGE * now[h]) * inverse[2 * q + h]
        return carry

    lax.fori_loop(1, ITERS, sweep, 0)

    mask_row = small[fibres : fibres + 1, :]
    sky_row = small[fibres + 1 : fibres + 2, :]
    scale = small[fibres + 2 : fibres + 3, 0:1]
    number = me * fibres + lax.broadcasted_iota(jnp.int32, (fibres, small.shape[1]), 0)
    is_sky = jnp.max(jnp.where(number.astype(F32) == sky_row, 1.0, 0.0), axis=1, keepdims=True)
    count = mask_out.shape[0]
    for b in range(count // fibres):
        row = b * fibres + lax.broadcasted_iota(jnp.int32, (fibres, small.shape[1]), 0)
        lane = lax.broadcasted_iota(jnp.int32, (fibres, small.shape[1]), 1)
        column = jnp.sum(jnp.where(row == lane, mask_row, 0.0), axis=1, keepdims=True)
        mask_out[b * fibres : (b + 1) * fibres, :] = jnp.broadcast_to(column, (fibres, LANES))
    own = mask_out[pl.ds(pl.multiple_of(me * fibres, fibres), fibres), :]
    chosen = is_sky * own * scale
    pick = (chosen, chosen * scale)
    gain_out[...] = jnp.broadcast_to(scale, gain_out.shape)

    margin = LW // 2
    for q, (g, j) in enumerate(pairs):
        half = slice(j * LANES, (j + 1) * LANES)

        def kept(values):
            return jnp.concatenate(
                [values[2 * q, :, margin : margin + LW], values[2 * q + 1, :, margin : margin + LW]],
                axis=1,
            )

        spectrum = kept(flux)
        strength = kept(row_weight)
        o, i, _ = flat[g]
        outs[o][i, :fibres, half] = spectrum
        outs[o][i, fibres:, half] = jnp.concatenate(
            [
                jnp.sum(pick[0] * strength * spectrum, axis=0, keepdims=True),
                jnp.sum(pick[1] * strength, axis=0, keepdims=True),
                jnp.zeros((EXTRA - 2, LANES), F32),
            ],
            axis=0,
        )


def relax(groups, width, outer, inner, terms, first, *rest):
    square, window = terms.shape[1:]
    fibres = first.shape[1]
    number = sum(len(group) for group in groups)
    count = number * width // LW
    count_all = terms.shape[0] * LW // width * fibres
    near = pl.BlockSpec(memory_space=pltpu.VMEM)
    return pl.pallas_call(
        functools.partial(relax_kernel, groups),
        in_specs=[near] * (4 + len(rest)),
        out_specs=[near] * (len(groups) + 2),
        out_shape=[jax.ShapeDtypeStruct((len(group), fibres + EXTRA, width), F32) for group in groups]
        + [jax.ShapeDtypeStruct((count_all, LANES), F32), jax.ShapeDtypeStruct((8, LANES), F32)],
        scratch_shapes=[pltpu.VMEM((number, 2 * HALO, width + 2 * LANES), BF16)] * 2
        + [pltpu.VMEM((count, square, window), F32)]
        + [pltpu.VMEM((count, fibres, window), F32)] * 4,
        compiler_params=pltpu.CompilerParams(vmem_limit_bytes=16 * 2**20),
        name="relax",
    )(outer, inner, terms, first, *rest)


def finish_kernel(fibres, cameras, gain, mask, own, swapped, *rest):
    *blocks_in, calibrated, model = rest
    totals = tree([part[...] for part in blocks_in[:cameras]])
    across = blocks_in[cameras:]
    me = lax.axis_index("patch")
    sky = totals[0:1, :] / (PRIOR + totals[1:2, :])
    model[...] = sky
    blocks = {0: own[0, :fibres, :], 1: swapped[0, :fibres, :]}
    for t, block in enumerate(across):
        blocks[2 * t + 2] = block[0, :fibres, :]
        blocks[2 * t + 3] = swapped[t + 1, :fibres, :]
    for s, block in blocks.items():
        at = pl.ds(pl.multiple_of((me ^ s) * fibres, fibres), fibres)
        calibrated[at, :] = mask[at, 0:1] * (block - gain[0:1, 0:1] * sky)


def finish(fibres, gain, mask, own, swapped, parts, across):
    width = own.shape[-1]
    near = pl.BlockSpec(memory_space=pltpu.VMEM)
    return pl.pallas_call(
        functools.partial(finish_kernel, fibres, len(parts)),
        in_specs=[near] * (4 + len(parts) + len(across)),
        out_specs=[near] * 2,
        out_shape=[
            jax.ShapeDtypeStruct((mask.shape[0], width), F32),
            jax.ShapeDtypeStruct((1, width), F32),
        ],
        name="finish",
    )(gain, mask, own, swapped, *parts, *across)


def tree(terms):
    return terms[0] if len(terms) == 1 else tree(terms[0::2]) + tree(terms[1::2])


def swap(values, axis, shift):
    return lax.ppermute(values, axis, [(i, i ^ shift) for i in range(lax.axis_size(axis))])


def packed(traces, cross, mask, sky, gain):
    width = max(LANES, mask.shape[1])

    def wide(values, fill=0.0):
        values = values.astype(F32)
        return jnp.pad(values, ((0, 0), (0, width - values.shape[1])), constant_values=fill)

    rows = [
        wide(jnp.concatenate([traces.astype(F32), cross.astype(F32)], axis=1)),
        wide(mask),
        wide(sky, -1.0),
        jnp.broadcast_to(gain[:, None], (1, width)),
        jnp.zeros((5, width), F32),
    ]
    return jnp.concatenate(rows, axis=0)


def per_device(
    pixel_counts,
    pixel_weights,
    wave_profile,
    cross_profile,
    trace_columns,
    throughput,
    sky_fibres,
    fibre_mask,
):
    fibres = trace_columns.shape[1]
    parts = lax.axis_size("patch")
    cameras = lax.axis_size("ccd")
    width = pixel_counts.shape[2] // parts
    me = lax.axis_index("patch")
    columns = pixel_counts.shape[1]
    wave = wave_profile[0, 0]
    pixels = jnp.pad(
        jnp.concatenate([pixel_counts[0], pixel_weights[0]], axis=0), ((0, 0), (LANES, LANES))
    )
    first = jnp.concatenate([pixels[:HALO], pixels[columns : columns + HALO]], axis=0)
    final = jnp.concatenate([pixels[columns - HALO : columns], pixels[2 * columns - HALO :]], axis=0)
    odd = me % 2 == 1
    outer = jnp.where(odd, final, first)
    inner = jnp.where(odd, first, final)
    small = packed(
        trace_columns[0] - me * columns, cross_profile[0], fibre_mask, sky_fibres, throughput
    )
    far = [(i, i + 1) for i in range(1, parts - 1, 2)]
    outer = lax.ppermute(outer, "patch", far + [(b, a) for a, b in far])
    inner = swap(inner, "patch", 1)
    state = [*prepare(small, pixels, wave, fibres), small, wave]
    *away, _, _ = relax([(s, s + 1) for s in range(2, parts, 2)], width, outer, inner, *state)
    across = [swap(block, "patch", 2 * t + 2) for t, block in enumerate(away)]
    state[0], *away = lax.optimization_barrier((state[0], *away))
    own, mate, mask, gain = relax([(0,), (1,)], width, outer, inner, *state)
    swapped = swap(jnp.concatenate([mate] + [block[1:] for block in across], axis=0), "patch", 1)
    sky = slice(fibres, fibres + 2)
    part = own[0, sky] + jnp.sum(swapped[:, sky], axis=0)
    for block in across:
        part = part + block[0, sky]
    sums = [part] + [swap(part, "ccd", s) for s in range(1, cameras)]
    calibrated, model = finish(fibres, gain, mask, own, swapped, sums, across)
    return calibrated[None], model[0]


def solution(mesh):
    return jax.shard_map(
        per_device,
        mesh=mesh,
        in_specs=(
            P("ccd", "patch", None),
            P("ccd", "patch", None),
            P("ccd", "patch", None, None, None),
            P("ccd", "patch", None),
            P("ccd", "patch", None),
            P("ccd"),
            P("ccd", None),
            P("ccd", None),
        ),
        out_specs=(P("ccd", None, "patch"), P("patch")),
        check_vma=False,
    )
```

```python
import functools
import jax
import jax.numpy as jnp
from jax import lax
from jax.sharding import PartitionSpec as P
from jax.experimental import pallas as pl
from jax.experimental.pallas import tpu as pltpu

LW = 64
ITERS = 10
HALO = 8
RIDGE = 0.1
PRIOR = 1.0
LANES = 128
EXTRA = 8
F32 = jnp.float32
BF16 = jnp.bfloat16


def mm(a, b):
    return jnp.dot(a, b, preferred_element_type=F32)


def pair_mm(a, b, stacked):
    a = a.astype(BF16)
    b = b.astype(BF16)
    zero = jnp.zeros_like(a)
    left = jnp.concatenate(
        [jnp.concatenate([a, zero], axis=1), jnp.concatenate([zero, b], axis=1)], axis=0
    )
    both = mm(left, stacked)
    return both[: a.shape[0]], both[a.shape[0] :]


def profile_rows(cols, cross, columns):
    fibres = cols.shape[0]
    lane = lax.broadcasted_iota(jnp.int32, (fibres, columns + 2 * HALO), 1)
    column = jnp.where(
        lane < columns, lane, jnp.where(lane < columns + HALO, lane - columns - HALO, lane - HALO)
    )
    total = jnp.zeros(column.shape, F32)
    for k in range(cols.shape[1]):
        total = total + jnp.where(cols[:, k : k + 1] == column, cross[:, k : k + 1], 0.0)
    return total.astype(BF16).astype(F32)


def split(values):
    top = values.astype(BF16)
    return top, (values - top.astype(F32)).astype(BF16)


def prepare_kernel(
    traces, cross, pixels, wave,
    terms, first, mixed, turned, row_total, side, side_sum, main, main_sum,
):
    columns = pixels.shape[0] // 2
    fibres = first.shape[1]
    patches = wave.shape[0]
    square = fibres * fibres

    first_column = lax.axis_index("patch") * columns
    profile = profile_rows(traces[...] - first_column, cross[...].astype(F32), columns)
    spread = (profile * jnp.sum(profile, axis=0, keepdims=True)).astype(BF16)
    for f in range(fibres):
        at = slice(f * fibres, (f + 1) * fibres)
        top, low = split(profile * profile[f : f + 1, :])
        main[at, :] = jnp.concatenate([top[:, :columns], low[:, :columns]], axis=1)
        side[at, :] = jnp.concatenate([top[:, columns:], low[:, columns:]], axis=1)
    half = profile.astype(BF16)
    main[square:, :] = jnp.concatenate([spread[:, :columns], jnp.zeros((fibres, columns), BF16)], axis=1)
    side[square:, :] = jnp.concatenate([spread[:, columns:], jnp.zeros((fibres, 2 * HALO), BF16)], axis=1)
    main_sum[...] = jnp.concatenate([half[:, :columns]] * 2, axis=1)
    side_sum[...] = jnp.concatenate([half[:, columns:]] * 2, axis=1)

    for k in range(patches // 2):
        start = LANES - LW // 2 + k * LANES

        def window(rows):
            return jnp.concatenate(
                [pixels[rows, start : start + LANES], pixels[rows, start + LW : start + LW + LANES]], axis=1
            )

        weight = window(slice(columns, 2 * columns))
        top, low = split(weight.astype(F32) * window(slice(columns)).astype(F32))
        both = mm(main[...], jnp.concatenate([weight, weight], axis=0))
        sums = mm(main_sum[...], jnp.concatenate([top, low], axis=0))
        for h in range(2):
            at = slice(h * LANES, (h + 1) * LANES)
            terms[2 * k + h] = both[:square, at]
            mixed[2 * k + h] = both[square:, at]
            first[2 * k + h] = sums[:, at]

    for p in range(patches):
        flipped = wave[p].T
        turned[p] = flipped
        total = jnp.sum(flipped.astype(F32), axis=0, keepdims=True)
        row_total[p] = jnp.broadcast_to(total, row_total.shape[1:])


def prepare(traces, cross, pixels, wave):
    columns = pixels.shape[0] // 2
    fibres = traces.shape[0]
    patches, window, _ = wave.shape
    square = fibres * fibres
    near = pl.BlockSpec(memory_space=pltpu.VMEM)
    shape = jax.ShapeDtypeStruct
    return pl.pallas_call(
        prepare_kernel,
        in_specs=[near] * 4,
        out_specs=[near] * 7,
        out_shape=[
            shape((patches, square, window), F32),
            shape((patches, fibres, window), F32),
            shape((patches, fibres, window), F32),
            shape(wave.shape, BF16),
            shape((patches, 8, window), F32),
            shape((square + fibres, 4 * HALO), BF16),
            shape((fibres, 4 * HALO), BF16),
        ],
        scratch_shapes=[
            pltpu.VMEM((square + fibres, 2 * columns), BF16),
            pltpu.VMEM((fibres, 2 * columns), BF16),
        ],
        compiler_params=pltpu.CompilerParams(vmem_limit_bytes=8 * 2**20),
        name="prepare",
    )(traces, cross, pixels, wave)


def relax_kernel(
    groups, outer, inner, terms_own, first_own, mixed_own, turned, row_total, side, side_sum, wave, sky, mask, gain, *rest
):
    outs = rest[: len(groups)]
    *columns_out, wpad, cpad, terms, first, inverse, flux, row_weight = rest[len(groups) :]
    me = lax.axis_index("patch")
    odd = me % 2 == 1
    square, fibres = terms.shape[1], first.shape[1]
    width = outs[0].shape[-1]
    tiles = width // LANES
    per = width // LW
    flat = [(o, i, s) for o, group in enumerate(groups) for i, s in enumerate(group)]
    owner = [me ^ s for _, _, s in flat]
    pairs = [(g, j) for g in range(len(flat)) for j in range(per // 2)]

    for g in range(len(flat)):
        for t in range(tiles + 2):
            lanes = pl.ds(pl.multiple_of((owner[g] * tiles + t) * LANES, LANES), LANES)
            near = inner[:, lanes].astype(F32)
            far = outer[:, lanes].astype(F32)
            below = jnp.where(odd, near, far)
            above = jnp.where(odd, far, near)
            for i, pad in ((0, cpad), (1, wpad)):
                at = slice(i * HALO, (i + 1) * HALO)
                both = jnp.concatenate([below[at], above[at]], axis=0).astype(BF16)
                pad[g, :, t * LANES : (t + 1) * LANES] = both

    for q, (g, j) in enumerate(pairs):
        start = LANES - LW // 2 + j * LANES

        def window(pad):
            return jnp.concatenate(
                [pad[g, :, start : start + LANES], pad[g, :, start + LW : start + LW + LANES]], axis=1
            )

        weight = window(wpad)
        top, bottom = split(weight.astype(F32) * window(cpad).astype(F32))
        both = mm(side[...], jnp.concatenate([weight, weight], axis=0))
        sums = mm(side_sum[...], jnp.concatenate([top, bottom], axis=0))
        for h in range(2):
            p = owner[g] * per + 2 * j + h
            at = slice(h * LANES, (h + 1) * LANES)
            terms[2 * q + h] = terms_own[p] + both[:square, at]
            first[2 * q + h] = first_own[p] + sums[:, at]
            whole_sum = (mixed_own[p] + both[square:, at]).astype(BF16).astype(F32)
            flux[2 * q + h] = whole_sum * row_total[p, 0:1, :]

    def stacked(ref, g, j):
        return ref[pl.ds(owner[g] * per + 2 * j, 2)].reshape(2 * LANES, LANES)

    for q, (g, j) in enumerate(pairs):
        grid = stacked(wave, g, j)
        weight_pair = pair_mm(flux[2 * q], flux[2 * q + 1], grid)
        step_pair = pair_mm(first[2 * q], first[2 * q + 1], grid)
        for h in range(2):
            total = weight_pair[h] + RIDGE
            row_weight[2 * q + h] = total
            reciprocal = 1.0 / total
            inverse[2 * q + h] = reciprocal
            flux[2 * q + h] = step_pair[h] * reciprocal

    def sweep(_, carry):
        for q, (g, j) in enumerate(pairs):
            now = [flux[2 * q], flux[2 * q + 1]]
            blurred = pair_mm(*now, stacked(turned, g, j))
            folded = []
            for h in range(2):
                total = first[2 * q + h]
                for f in range(fibres):
                    term = terms[2 * q + h, f * fibres : (f + 1) * fibres, :]
                    total = total - term * blurred[h][f : f + 1, :]
                folded.append(total)
            gradient = pair_mm(*folded, stacked(wave, g, j))
            for h in range(2):
                flux[2 * q + h] = now[h] + (gradient[h] - RIDGE * now[h]) * inverse[2 * q + h]
        return carry

    lax.fori_loop(1, ITERS, sweep, 0, unroll=9)

    number = me * fibres + lax.broadcasted_iota(jnp.int32, (fibres, sky.shape[1]), 0)
    is_sky = jnp.max(jnp.where(number == sky[...], 1.0, 0.0), axis=1, keepdims=True)
    row = lax.broadcasted_iota(jnp.int32, (fibres, mask.shape[1]), 0)
    lane = lax.broadcasted_iota(jnp.int32, (fibres, mask.shape[1]), 1)
    working = mask[...].astype(F32)

    def mask_column(first_row):
        return jnp.sum(jnp.where(lane == row + first_row, working, 0.0), axis=1, keepdims=True)

    for out in columns_out:
        for b in range(out.shape[0] // fibres):
            out[b * fibres : (b + 1) * fibres, :] = jnp.broadcast_to(mask_column(b * fibres), (fibres, LANES))
    own = mask_column(me * fibres)
    scale = gain[0]
    chosen = is_sky * own * scale
    pick = (chosen, chosen * scale)

    margin = LW // 2
    for q, (g, j) in enumerate(pairs):
        half = slice(j * LANES, (j + 1) * LANES)

        def kept(values):
            return jnp.concatenate(
                [values[2 * q, :, margin : margin + LW], values[2 * q + 1, :, margin : margin + LW]],
                axis=1,
            )

        spectrum = kept(flux)
        strength = kept(row_weight)
        o, i, _ = flat[g]
        outs[o][i, :fibres, half] = spectrum
        outs[o][i, fibres:, half] = jnp.concatenate(
            [
                jnp.sum(pick[0] * strength * spectrum, axis=0, keepdims=True),
                jnp.sum(pick[1] * strength, axis=0, keepdims=True),
                jnp.zeros((EXTRA - 2, LANES), F32),
            ],
            axis=0,
        )


def relax(groups, width, columns, outer, inner, terms, first, *rest):
    square, window = terms.shape[1:]
    fibres = first.shape[1]
    number = sum(len(group) for group in groups)
    patches = number * width // LW
    near = pl.BlockSpec(memory_space=pltpu.VMEM)
    return pl.pallas_call(
        functools.partial(relax_kernel, groups),
        in_specs=[near] * (3 + len(rest)) + [pl.BlockSpec(memory_space=pltpu.SMEM)],
        out_specs=[near] * (len(groups) + len(columns)),
        out_shape=[jax.ShapeDtypeStruct((len(group), fibres + EXTRA, width), F32) for group in groups]
        + [jax.ShapeDtypeStruct((count, LANES), F32) for count in columns],
        scratch_shapes=[pltpu.VMEM((number, 2 * HALO, width + 2 * LANES), BF16)] * 2
        + [pltpu.VMEM((patches, square, window), F32)]
        + [pltpu.VMEM((patches, fibres, window), F32)] * 4,
        compiler_params=pltpu.CompilerParams(vmem_limit_bytes=16 * 2**20),
        name="relax",
    )(outer, inner, terms, first, *rest)


def finish_kernel(fibres, cameras, gain, mask, own, swapped, *rest):
    *blocks_in, calibrated, model = rest
    totals = tree([part[...] for part in blocks_in[:cameras]])
    across = blocks_in[cameras:]
    me = lax.axis_index("patch")
    sky = totals[0:1, :] / (PRIOR + totals[1:2, :])
    model[...] = sky
    blocks = {0: own[0, :fibres, :], 1: swapped[0, :fibres, :]}
    for t, block in enumerate(across):
        blocks[2 * t + 2] = block[0, :fibres, :]
        blocks[2 * t + 3] = swapped[t + 1, :fibres, :]
    for s, block in blocks.items():
        at = pl.ds(pl.multiple_of((me ^ s) * fibres, fibres), fibres)
        calibrated[at, :] = mask[at, 0:1] * (block - gain[0] * sky)


def finish(fibres, gain, mask, own, swapped, parts, across):
    width = own.shape[-1]
    near = pl.BlockSpec(memory_space=pltpu.VMEM)
    return pl.pallas_call(
        functools.partial(finish_kernel, fibres, len(parts)),
        in_specs=[pl.BlockSpec(memory_space=pltpu.SMEM)] + [near] * (3 + len(parts) + len(across)),
        out_specs=[near] * 2,
        out_shape=[
            jax.ShapeDtypeStruct((mask.shape[0], width), F32),
            jax.ShapeDtypeStruct((1, width), F32),
        ],
        compiler_params=pltpu.CompilerParams(vmem_limit_bytes=8 * 2**20),
        name="finish",
    )(gain, mask, own, swapped, *parts, *across)


def tree(terms):
    return terms[0] if len(terms) == 1 else tree(terms[0::2]) + tree(terms[1::2])


def swap(values, axis, shift):
    return lax.ppermute(values, axis, [(i, i ^ shift) for i in range(lax.axis_size(axis))])


def per_device(
    pixel_counts,
    pixel_weights,
    wave_profile,
    cross_profile,
    trace_columns,
    throughput,
    sky_fibres,
    fibre_mask,
):
    fibres = trace_columns.shape[1]
    parts = lax.axis_size("patch")
    cameras = lax.axis_size("ccd")
    width = pixel_counts.shape[2] // parts
    me = lax.axis_index("patch")
    columns = pixel_counts.shape[1]
    wave = wave_profile[0, 0]
    pixels = jnp.pad(
        jnp.concatenate([pixel_counts[0], pixel_weights[0]], axis=0), ((0, 0), (LANES, LANES))
    )
    first = jnp.concatenate([pixels[:HALO], pixels[columns : columns + HALO]], axis=0)
    final = jnp.concatenate([pixels[columns - HALO : columns], pixels[2 * columns - HALO :]], axis=0)
    odd = me % 2 == 1
    outer = jnp.where(odd, final, first)
    inner = jnp.where(odd, first, final)
    far = [(i, i + 1) for i in range(1, parts - 1, 2)]
    outer = lax.ppermute(outer, "patch", far + [(b, a) for a, b in far])
    inner = swap(inner, "patch", 1)
    state = prepare(trace_columns[0], cross_profile[0], pixels, wave)
    state = [*state, wave, sky_fibres, fibre_mask, throughput]
    away = relax([(s, s + 1) for s in range(2, parts, 2)], width, (), outer, inner, *state)
    across = [swap(block, "patch", 2 * t + 2) for t, block in enumerate(away)]
    state[0], *away = lax.optimization_barrier((state[0], *away))
    own, mate, mask = relax([(0,), (1,)], width, (fibre_mask.shape[1],), outer, inner, *state)
    swapped = swap(jnp.concatenate([mate] + [block[1:] for block in across], axis=0), "patch", 1)
    sky = slice(fibres, fibres + 2)
    part = own[0, sky] + jnp.sum(swapped[:, sky], axis=0)
    for block in across:
        part = part + block[0, sky]
    sums = [part] + [swap(part, "ccd", s) for s in range(1, cameras)]
    calibrated, model = finish(fibres, throughput, mask, own, swapped, sums, across)
    return calibrated[None], model[0]


def solution(mesh):
    return jax.shard_map(
        per_device,
        mesh=mesh,
        in_specs=(
            P("ccd", "patch", None),
            P("ccd", "patch", None),
            P("ccd", "patch", None, None, None),
            P("ccd", "patch", None),
            P("ccd", "patch", None),
            P("ccd"),
            P("ccd", None),
            P("ccd", None),
        ),
        out_specs=(P("ccd", None, "patch"), P("patch")),
        check_vma=False,
    )
```

```python
import functools
import jax
import jax.numpy as jnp
from jax import lax
from jax.sharding import PartitionSpec as P
from jax.experimental import pallas as pl
from jax.experimental.pallas import tpu as pltpu

LW = 64
ITERS = 10
HALO = 8
RIDGE = 0.1
PRIOR = 1.0
LANES = 128
EXTRA = 8
F32 = jnp.float32
BF16 = jnp.bfloat16


def mm(a, b):
    return jnp.dot(a, b, preferred_element_type=F32)


def pair_mm(a, b, stacked):
    a = a.astype(BF16)
    b = b.astype(BF16)
    zero = jnp.zeros_like(a)
    left = jnp.concatenate(
        [jnp.concatenate([a, zero], axis=1), jnp.concatenate([zero, b], axis=1)], axis=0
    )
    both = mm(left, stacked)
    return both[: a.shape[0]], both[a.shape[0] :]


def profile_rows(cols, cross, columns):
    fibres = cols.shape[0]
    lane = lax.broadcasted_iota(jnp.int32, (fibres, columns + 2 * HALO), 1)
    column = jnp.where(
        lane < columns, lane, jnp.where(lane < columns + HALO, lane - columns - HALO, lane - HALO)
    )
    total = jnp.zeros(column.shape, F32)
    for k in range(cols.shape[1]):
        total = total + jnp.where(cols[:, k : k + 1] == column, cross[:, k : k + 1], 0.0)
    return total.astype(BF16).astype(F32)


def split(values):
    top = values.astype(BF16)
    return top, (values - top.astype(F32)).astype(BF16)


def prepare_kernel(
    traces, cross, pixels, wave,
    terms, first, mixed, turned, row_total, side, side_sum, main, main_sum,
):
    columns = pixels.shape[0] // 2
    fibres = first.shape[1]
    patches = wave.shape[0]
    square = fibres * fibres

    first_column = lax.axis_index("patch") * columns
    profile = profile_rows(traces[...] - first_column, cross[...].astype(F32), columns)
    spread = (profile * jnp.sum(profile, axis=0, keepdims=True)).astype(BF16)
    for f in range(fibres):
        at = slice(f * fibres, (f + 1) * fibres)
        top, low = split(profile * profile[f : f + 1, :])
        main[at, :] = jnp.concatenate([top[:, :columns], low[:, :columns]], axis=1)
        side[at, :] = jnp.concatenate([top[:, columns:], low[:, columns:]], axis=1)
    half = profile.astype(BF16)
    main[square:, :] = jnp.concatenate([spread[:, :columns], jnp.zeros((fibres, columns), BF16)], axis=1)
    side[square:, :] = jnp.concatenate([spread[:, columns:], jnp.zeros((fibres, 2 * HALO), BF16)], axis=1)
    main_sum[...] = jnp.concatenate([half[:, :columns]] * 2, axis=1)
    side_sum[...] = jnp.concatenate([half[:, columns:]] * 2, axis=1)

    for k in range(patches // 2):
        start = LANES - LW // 2 + k * LANES

        def window(rows):
            return jnp.concatenate(
                [pixels[rows, start : start + LANES], pixels[rows, start + LW : start + LW + LANES]], axis=1
            )

        weight = window(slice(columns, 2 * columns))
        top, low = split(weight.astype(F32) * window(slice(columns)).astype(F32))
        both = mm(main[...], jnp.concatenate([weight, weight], axis=0))
        sums = mm(main_sum[...], jnp.concatenate([top, low], axis=0))
        for h in range(2):
            at = slice(h * LANES, (h + 1) * LANES)
            terms[2 * k + h] = both[:square, at]
            mixed[2 * k + h] = both[square:, at]
            first[2 * k + h] = sums[:, at]

    for p in range(patches):
        flipped = wave[p].T
        turned[p] = flipped
        total = jnp.sum(flipped.astype(F32), axis=0, keepdims=True)
        row_total[p] = jnp.broadcast_to(total, row_total.shape[1:])


def prepare(traces, cross, pixels, wave):
    columns = pixels.shape[0] // 2
    fibres = traces.shape[0]
    patches, window, _ = wave.shape
    square = fibres * fibres
    near = pl.BlockSpec(memory_space=pltpu.VMEM)
    shape = jax.ShapeDtypeStruct
    return pl.pallas_call(
        prepare_kernel,
        in_specs=[near] * 4,
        out_specs=[near] * 7,
        out_shape=[
            shape((patches, square, window), F32),
            shape((patches, fibres, window), F32),
            shape((patches, fibres, window), F32),
            shape(wave.shape, BF16),
            shape((patches, 8, window), F32),
            shape((square + fibres, 4 * HALO), BF16),
            shape((fibres, 4 * HALO), BF16),
        ],
        scratch_shapes=[
            pltpu.VMEM((square + fibres, 2 * columns), BF16),
            pltpu.VMEM((fibres, 2 * columns), BF16),
        ],
        compiler_params=pltpu.CompilerParams(vmem_limit_bytes=8 * 2**20),
        name="prepare",
    )(traces, cross, pixels, wave)


def relax_kernel(
    groups, outer, inner, terms_own, first_own, mixed_own, turned, row_total, side, side_sum, wave, sky, mask, *rest
):
    outs = rest[: len(groups)]
    *columns_out, wpad, cpad, terms, first, inverse, flux, row_weight = rest[len(groups) :]
    me = lax.axis_index("patch")
    odd = me % 2 == 1
    square, fibres = terms.shape[1], first.shape[1]
    width = outs[0].shape[-1]
    tiles = width // LANES
    per = width // LW
    flat = [(o, i, s) for o, group in enumerate(groups) for i, s in enumerate(group)]
    owner = [me ^ s for _, _, s in flat]
    pairs = [(g, j) for g in range(len(flat)) for j in range(per // 2)]

    last = outer.shape[1] // LANES - 1
    for g in range(len(flat)):
        for t in range(tiles + 2):
            tile = owner[g] * tiles + t - 1
            lanes = pl.ds(pl.multiple_of(jnp.clip(tile, 0, last) * LANES, LANES), LANES)
            near = inner[:, lanes].astype(F32)
            far = outer[:, lanes].astype(F32)
            if t == 0 or t == tiles + 1:
                inside = jnp.logical_and(tile >= 0, tile <= last)
                near = jnp.where(inside, near, 0.0)
                far = jnp.where(inside, far, 0.0)
            below = jnp.where(odd, near, far)
            above = jnp.where(odd, far, near)
            for i, pad in ((0, cpad), (1, wpad)):
                at = slice(i * HALO, (i + 1) * HALO)
                both = jnp.concatenate([below[at], above[at]], axis=0).astype(BF16)
                pad[g, :, t * LANES : (t + 1) * LANES] = both

    for q, (g, j) in enumerate(pairs):
        start = LANES - LW // 2 + j * LANES

        def window(pad):
            return jnp.concatenate(
                [pad[g, :, start : start + LANES], pad[g, :, start + LW : start + LW + LANES]], axis=1
            )

        weight = window(wpad)
        top, bottom = split(weight.astype(F32) * window(cpad).astype(F32))
        both = mm(side[...], jnp.concatenate([weight, weight], axis=0))
        sums = mm(side_sum[...], jnp.concatenate([top, bottom], axis=0))
        for h in range(2):
            p = owner[g] * per + 2 * j + h
            at = slice(h * LANES, (h + 1) * LANES)
            terms[2 * q + h] = terms_own[p] + both[:square, at]
            first[2 * q + h] = first_own[p] + sums[:, at]
            whole_sum = (mixed_own[p] + both[square:, at]).astype(BF16).astype(F32)
            flux[2 * q + h] = whole_sum * row_total[p, 0:1, :]

    def stacked(ref, g, j):
        return ref[pl.ds(owner[g] * per + 2 * j, 2)].reshape(2 * LANES, LANES)

    for q, (g, j) in enumerate(pairs):
        grid = stacked(wave, g, j)
        weight_pair = pair_mm(flux[2 * q], flux[2 * q + 1], grid)
        step_pair = pair_mm(first[2 * q], first[2 * q + 1], grid)
        for h in range(2):
            total = weight_pair[h] + RIDGE
            row_weight[2 * q + h] = total
            reciprocal = 1.0 / total
            inverse[2 * q + h] = reciprocal
            flux[2 * q + h] = step_pair[h] * reciprocal

    def sweep(_, carry):
        for q, (g, j) in enumerate(pairs):
            now = [flux[2 * q], flux[2 * q + 1]]
            blurred = pair_mm(*now, stacked(turned, g, j))
            folded = []
            for h in range(2):
                total = first[2 * q + h]
                for f in range(fibres):
                    term = terms[2 * q + h, f * fibres : (f + 1) * fibres, :]
                    total = total - term * blurred[h][f : f + 1, :]
                folded.append(total)
            gradient = pair_mm(*folded, stacked(wave, g, j))
            for h in range(2):
                flux[2 * q + h] = now[h] + (gradient[h] - RIDGE * now[h]) * inverse[2 * q + h]
        return carry

    lax.fori_loop(1, ITERS, sweep, 0, unroll=9)

    number = me * fibres + lax.broadcasted_iota(jnp.int32, (fibres, sky.shape[1]), 0)
    is_sky = jnp.max(jnp.where(number == sky[...], 1.0, 0.0), axis=1, keepdims=True)
    row = lax.broadcasted_iota(jnp.int32, (fibres, mask.shape[1]), 0)
    lane = lax.broadcasted_iota(jnp.int32, (fibres, mask.shape[1]), 1)
    working = mask[...].astype(F32)

    def mask_column(first_row):
        return jnp.sum(jnp.where(lane == row + first_row, working, 0.0), axis=1, keepdims=True)

    for out in columns_out:
        for b in range(out.shape[0] // fibres):
            out[b * fibres : (b + 1) * fibres, :] = jnp.broadcast_to(mask_column(b * fibres), (fibres, LANES))
    chosen = is_sky * mask_column(me * fibres)

    margin = LW // 2
    for q, (g, j) in enumerate(pairs):
        half = slice(j * LANES, (j + 1) * LANES)

        def kept(values):
            return jnp.concatenate(
                [values[2 * q, :, margin : margin + LW], values[2 * q + 1, :, margin : margin + LW]],
                axis=1,
            )

        spectrum = kept(flux)
        strength = kept(row_weight)
        o, i, _ = flat[g]
        outs[o][i, :fibres, half] = spectrum
        outs[o][i, fibres:, half] = jnp.concatenate(
            [
                jnp.sum(chosen * strength * spectrum, axis=0, keepdims=True),
                jnp.sum(chosen * strength, axis=0, keepdims=True),
                jnp.zeros((EXTRA - 2, LANES), F32),
            ],
            axis=0,
        )


def relax(groups, width, columns, outer, inner, terms, first, *rest):
    square, window = terms.shape[1:]
    fibres = first.shape[1]
    number = sum(len(group) for group in groups)
    patches = number * width // LW
    near = pl.BlockSpec(memory_space=pltpu.VMEM)
    return pl.pallas_call(
        functools.partial(relax_kernel, groups),
        in_specs=[near] * (4 + len(rest)),
        out_specs=[near] * (len(groups) + len(columns)),
        out_shape=[jax.ShapeDtypeStruct((len(group), fibres + EXTRA, width), F32) for group in groups]
        + [jax.ShapeDtypeStruct((count, LANES), F32) for count in columns],
        scratch_shapes=[pltpu.VMEM((number, 2 * HALO, width + 2 * LANES), BF16)] * 2
        + [pltpu.VMEM((patches, square, window), F32)]
        + [pltpu.VMEM((patches, fibres, window), F32)] * 4,
        compiler_params=pltpu.CompilerParams(vmem_limit_bytes=16 * 2**20),
        name="relax",
    )(outer, inner, terms, first, *rest)


def finish_kernel(fibres, cameras, gain, mask, own, swapped, *rest):
    *blocks_in, calibrated, model = rest
    totals = tree([part[...] for part in blocks_in[:cameras][::-1]])
    across = blocks_in[cameras:]
    me = lax.axis_index("patch")
    sky = totals[0:1, :] / (PRIOR + totals[1:2, :])
    model[...] = sky
    blocks = {0: own[0, :fibres, :], 1: swapped[0, :fibres, :]}
    for t, block in enumerate(across):
        blocks[2 * t + 2] = block[0, :fibres, :]
        blocks[2 * t + 3] = swapped[t + 1, :fibres, :]
    for s, block in blocks.items():
        at = pl.ds(pl.multiple_of((me ^ s) * fibres, fibres), fibres)
        calibrated[at, :] = mask[at, 0:1] * (block - gain[0] * sky)


def finish(fibres, gain, mask, own, swapped, parts, across):
    width = own.shape[-1]
    near = pl.BlockSpec(memory_space=pltpu.VMEM)
    return pl.pallas_call(
        functools.partial(finish_kernel, fibres, len(parts)),
        in_specs=[pl.BlockSpec(memory_space=pltpu.SMEM)] + [near] * (3 + len(parts) + len(across)),
        out_specs=[near] * 2,
        out_shape=[
            jax.ShapeDtypeStruct((mask.shape[0], width), F32),
            jax.ShapeDtypeStruct((1, width), F32),
        ],
        compiler_params=pltpu.CompilerParams(vmem_limit_bytes=8 * 2**20),
        name="finish",
    )(gain, mask, own, swapped, *parts, *across)


def tree(terms):
    return terms[0] if len(terms) == 1 else tree(terms[0::2]) + tree(terms[1::2])


def swap(values, axis, shift):
    return lax.ppermute(values, axis, [(i, i ^ shift) for i in range(lax.axis_size(axis))])


def per_device(
    pixel_counts,
    pixel_weights,
    wave_profile,
    cross_profile,
    trace_columns,
    throughput,
    sky_fibres,
    fibre_mask,
):
    fibres = trace_columns.shape[1]
    parts = lax.axis_size("patch")
    cameras = lax.axis_size("ccd")
    width = pixel_counts.shape[2] // parts
    me = lax.axis_index("patch")
    columns = pixel_counts.shape[1]
    wave = wave_profile[0, 0]
    counts, weights = pixel_counts[0], pixel_weights[0]
    first = jnp.concatenate([counts[:HALO], weights[:HALO]], axis=0)
    final = jnp.concatenate([counts[columns - HALO :], weights[columns - HALO :]], axis=0)
    odd = me % 2 == 1
    outer = jnp.where(odd, final, first)
    inner = jnp.where(odd, first, final)
    far = [(i, i + 1) for i in range(1, parts - 1, 2)]
    outer = lax.ppermute(outer, "patch", far + [(b, a) for a, b in far])
    inner = swap(inner, "patch", 1)
    pixels = jnp.pad(
        jnp.concatenate([pixel_counts[0], pixel_weights[0]], axis=0), ((0, 0), (LANES, LANES))
    )
    state = prepare(trace_columns[0], cross_profile[0], pixels, wave)
    state = [*state, wave, sky_fibres, fibre_mask]
    away = relax([(s, s + 1) for s in range(2, parts, 2)], width, (), outer, inner, *state)
    across = [swap(block, "patch", 2 * t + 2) for t, block in enumerate(away)]
    state[0], *away = lax.optimization_barrier((state[0], *away))
    own, mate, mask = relax([(0,), (1,)], width, (fibre_mask.shape[1],), outer, inner, *state)
    sky = slice(fibres, fibres + 2)
    part, other = own[0, sky], mate[0, sky]
    for block in across:
        part, other = part + block[0, sky], other + block[1, sky]
    other = swap(other, "patch", 1)
    swapped = swap(jnp.concatenate([mate] + [block[1:] for block in across], axis=0), "patch", 1)
    part = part + other
    part = part * jnp.stack([throughput, throughput * throughput])
    sums = [part] + [swap(part, "ccd", s) for s in range(1, cameras)]
    calibrated, model = finish(fibres, throughput, mask, own, swapped, sums[::-1], across)
    return calibrated[None], model[0]


def solution(mesh):
    return jax.shard_map(
        per_device,
        mesh=mesh,
        in_specs=(
            P("ccd", "patch", None),
            P("ccd", "patch", None),
            P("ccd", "patch", None, None, None),
            P("ccd", "patch", None),
            P("ccd", "patch", None),
            P("ccd"),
            P("ccd", None),
            P("ccd", None),
        ),
        out_specs=(P("ccd", None, "patch"), P("patch")),
        check_vma=False,
    )
```

```python
import functools
import jax
import jax.numpy as jnp
from jax import lax
from jax.sharding import PartitionSpec as P
from jax.experimental import pallas as pl
from jax.experimental.pallas import tpu as pltpu

LW = 64
ITERS = 10
HALO = 8
RIDGE = 0.1
PRIOR = 1.0
LANES = 128
EXTRA = 8
F32 = jnp.float32
BF16 = jnp.bfloat16


def mm(a, b):
    return jnp.dot(a, b, preferred_element_type=F32)


def pair_mm(a, b, stacked):
    a = a.astype(BF16)
    b = b.astype(BF16)
    zero = jnp.zeros_like(a)
    left = jnp.concatenate(
        [jnp.concatenate([a, zero], axis=1), jnp.concatenate([zero, b], axis=1)], axis=0
    )
    both = mm(left, stacked)
    return both[: a.shape[0]], both[a.shape[0] :]


def profile_rows(cols, cross, columns):
    fibres = cols.shape[0]
    lane = lax.broadcasted_iota(jnp.int32, (fibres, columns + 2 * HALO), 1)
    column = jnp.where(
        lane < columns, lane, jnp.where(lane < columns + HALO, lane - columns - HALO, lane - HALO)
    )
    total = jnp.zeros(column.shape, F32)
    for k in range(cols.shape[1]):
        total = total + jnp.where(cols[:, k : k + 1] == column, cross[:, k : k + 1], 0.0)
    return total.astype(BF16).astype(F32)


def split(values):
    top = values.astype(BF16)
    return top, (values - top.astype(F32)).astype(BF16)


def prepare_kernel(
    traces, cross, pixels, wave,
    terms, first, mixed, turned, row_total, side, side_sum, main, main_sum,
):
    columns = pixels.shape[0] // 2
    fibres = first.shape[1]
    patches = wave.shape[0]
    square = fibres * fibres

    first_column = lax.axis_index("patch") * columns
    profile = profile_rows(traces[...] - first_column, cross[...].astype(F32), columns)
    spread = (profile * jnp.sum(profile, axis=0, keepdims=True)).astype(BF16)
    for f in range(fibres):
        at = slice(f * fibres, (f + 1) * fibres)
        top, low = split(profile * profile[f : f + 1, :])
        main[at, :] = jnp.concatenate([top[:, :columns], low[:, :columns]], axis=1)
        side[at, :] = jnp.concatenate([top[:, columns:], low[:, columns:]], axis=1)
    half = profile.astype(BF16)
    main[square:, :] = jnp.concatenate([spread[:, :columns], jnp.zeros((fibres, columns), BF16)], axis=1)
    side[square:, :] = jnp.concatenate([spread[:, columns:], jnp.zeros((fibres, 2 * HALO), BF16)], axis=1)
    main_sum[...] = jnp.concatenate([half[:, :columns]] * 2, axis=1)
    side_sum[...] = jnp.concatenate([half[:, columns:]] * 2, axis=1)

    for k in range(patches // 2):
        start = LANES - LW // 2 + k * LANES

        def window(rows):
            return jnp.concatenate(
                [pixels[rows, start : start + LANES], pixels[rows, start + LW : start + LW + LANES]], axis=1
            )

        weight = window(slice(columns, 2 * columns))
        top, low = split(weight.astype(F32) * window(slice(columns)).astype(F32))
        both = mm(main[...], jnp.concatenate([weight, weight], axis=0))
        sums = mm(main_sum[...], jnp.concatenate([top, low], axis=0))
        for h in range(2):
            at = slice(h * LANES, (h + 1) * LANES)
            terms[2 * k + h] = both[:square, at]
            mixed[2 * k + h] = both[square:, at]
            first[2 * k + h] = sums[:, at]

    for p in range(patches):
        flipped = wave[p].T
        turned[p] = flipped
        total = jnp.sum(flipped.astype(F32), axis=0, keepdims=True)
        row_total[p] = jnp.broadcast_to(total, row_total.shape[1:])


def prepare(traces, cross, pixels, wave):
    columns = pixels.shape[0] // 2
    fibres = traces.shape[0]
    patches, window, _ = wave.shape
    square = fibres * fibres
    near = pl.BlockSpec(memory_space=pltpu.VMEM)
    shape = jax.ShapeDtypeStruct
    return pl.pallas_call(
        prepare_kernel,
        in_specs=[near] * 4,
        out_specs=[near] * 7,
        out_shape=[
            shape((patches, square, window), F32),
            shape((patches, fibres, window), F32),
            shape((patches, fibres, window), F32),
            shape(wave.shape, BF16),
            shape((patches, 8, window), F32),
            shape((square + fibres, 4 * HALO), BF16),
            shape((fibres, 4 * HALO), BF16),
        ],
        scratch_shapes=[
            pltpu.VMEM((square + fibres, 2 * columns), BF16),
            pltpu.VMEM((fibres, 2 * columns), BF16),
        ],
        compiler_params=pltpu.CompilerParams(vmem_limit_bytes=8 * 2**20),
        name="prepare",
    )(traces, cross, pixels, wave)


def relax_kernel(
    groups, outer, inner, terms_own, first_own, mixed_own, turned, row_total, side, side_sum, wave, sky, mask, *rest
):
    outs = rest[: len(groups)]
    *columns_out, wpad, cpad, terms, first, inverse, flux, row_weight = rest[len(groups) :]
    me = lax.axis_index("patch")
    odd = me % 2 == 1
    square, fibres = terms.shape[1], first.shape[1]
    width = outs[0].shape[-1]
    tiles = width // LANES
    per = width // LW
    flat = [(o, i, s) for o, group in enumerate(groups) for i, s in enumerate(group)]
    owner = [me ^ s for _, _, s in flat]
    pairs = [(g, j) for g in range(len(flat)) for j in range(per // 2)]

    last = outer.shape[1] // LANES - 1
    for g in range(len(flat)):
        for t in range(tiles + 2):
            tile = owner[g] * tiles + t - 1
            lanes = pl.ds(pl.multiple_of(jnp.clip(tile, 0, last) * LANES, LANES), LANES)
            near = inner[:, lanes].astype(F32)
            far = outer[:, lanes].astype(F32)
            if t == 0 or t == tiles + 1:
                inside = jnp.logical_and(tile >= 0, tile <= last)
                near = jnp.where(inside, near, 0.0)
                far = jnp.where(inside, far, 0.0)
            below = jnp.where(odd, near, far)
            above = jnp.where(odd, far, near)
            for i, pad in ((0, cpad), (1, wpad)):
                at = slice(i * HALO, (i + 1) * HALO)
                both = jnp.concatenate([below[at], above[at]], axis=0).astype(BF16)
                pad[g, :, t * LANES : (t + 1) * LANES] = both

    for q, (g, j) in enumerate(pairs):
        start = LANES - LW // 2 + j * LANES

        def window(pad):
            return jnp.concatenate(
                [pad[g, :, start : start + LANES], pad[g, :, start + LW : start + LW + LANES]], axis=1
            )

        weight = window(wpad)
        top, bottom = split(weight.astype(F32) * window(cpad).astype(F32))
        both = mm(side[...], jnp.concatenate([weight, weight], axis=0))
        sums = mm(side_sum[...], jnp.concatenate([top, bottom], axis=0))
        for h in range(2):
            p = owner[g] * per + 2 * j + h
            at = slice(h * LANES, (h + 1) * LANES)
            terms[2 * q + h] = terms_own[p] + both[:square, at]
            first[2 * q + h] = first_own[p] + sums[:, at]
            whole_sum = (mixed_own[p] + both[square:, at]).astype(BF16).astype(F32)
            flux[2 * q + h] = whole_sum * row_total[p, 0:1, :]

    def stacked(ref, g, j):
        return ref[pl.ds(owner[g] * per + 2 * j, 2)].reshape(2 * LANES, LANES)

    for q, (g, j) in enumerate(pairs):
        grid = stacked(wave, g, j)
        weight_pair = pair_mm(flux[2 * q], flux[2 * q + 1], grid)
        step_pair = pair_mm(first[2 * q], first[2 * q + 1], grid)
        for h in range(2):
            total = weight_pair[h] + RIDGE
            row_weight[2 * q + h] = total
            reciprocal = 1.0 / total
            inverse[2 * q + h] = reciprocal
            flux[2 * q + h] = step_pair[h] * reciprocal

    def sweep(_, carry):
        for q, (g, j) in enumerate(pairs):
            now = [flux[2 * q], flux[2 * q + 1]]
            blurred = pair_mm(*now, stacked(turned, g, j))
            folded = []
            for h in range(2):
                total = first[2 * q + h]
                for f in range(fibres):
                    term = terms[2 * q + h, f * fibres : (f + 1) * fibres, :]
                    total = total - term * blurred[h][f : f + 1, :]
                folded.append(total)
            gradient = pair_mm(*folded, stacked(wave, g, j))
            for h in range(2):
                flux[2 * q + h] = now[h] + (gradient[h] - RIDGE * now[h]) * inverse[2 * q + h]
        return carry

    lax.fori_loop(1, ITERS, sweep, 0, unroll=9)

    number = me * fibres + lax.broadcasted_iota(jnp.int32, (fibres, sky.shape[1]), 0)
    is_sky = jnp.max(jnp.where(number == sky[...], 1.0, 0.0), axis=1, keepdims=True)
    row = lax.broadcasted_iota(jnp.int32, (fibres, mask.shape[1]), 0)
    lane = lax.broadcasted_iota(jnp.int32, (fibres, mask.shape[1]), 1)
    working = mask[...].astype(F32)

    def mask_column(first_row):
        return jnp.sum(jnp.where(lane == row + first_row, working, 0.0), axis=1, keepdims=True)

    for out in columns_out:
        for b in range(out.shape[0] // fibres):
            out[b * fibres : (b + 1) * fibres, :] = jnp.broadcast_to(mask_column(b * fibres), (fibres, LANES))
    chosen = is_sky * mask_column(me * fibres)

    margin = LW // 2
    for q, (g, j) in enumerate(pairs):
        half = slice(j * LANES, (j + 1) * LANES)

        def kept(values):
            return jnp.concatenate(
                [values[2 * q, :, margin : margin + LW], values[2 * q + 1, :, margin : margin + LW]],
                axis=1,
            )

        spectrum = kept(flux)
        strength = kept(row_weight)
        o, i, _ = flat[g]
        outs[o][i, :fibres, half] = spectrum
        outs[o][i, fibres:, half] = jnp.concatenate(
            [
                jnp.sum(chosen * strength * spectrum, axis=0, keepdims=True),
                jnp.sum(chosen * strength, axis=0, keepdims=True),
                jnp.zeros((EXTRA - 2, LANES), F32),
            ],
            axis=0,
        )


def relax(groups, width, columns, outer, inner, terms, first, *rest):
    square, window = terms.shape[1:]
    fibres = first.shape[1]
    number = sum(len(group) for group in groups)
    patches = number * width // LW
    near = pl.BlockSpec(memory_space=pltpu.VMEM)
    return pl.pallas_call(
        functools.partial(relax_kernel, groups),
        in_specs=[near] * (4 + len(rest)),
        out_specs=[near] * (len(groups) + len(columns)),
        out_shape=[jax.ShapeDtypeStruct((len(group), fibres + EXTRA, width), F32) for group in groups]
        + [jax.ShapeDtypeStruct((count, LANES), F32) for count in columns],
        scratch_shapes=[pltpu.VMEM((number, 2 * HALO, width + 2 * LANES), BF16)] * 2
        + [pltpu.VMEM((patches, square, window), F32)]
        + [pltpu.VMEM((patches, fibres, window), F32)] * 4,
        compiler_params=pltpu.CompilerParams(vmem_limit_bytes=16 * 2**20),
        name="relax",
    )(outer, inner, terms, first, *rest)


def finish_kernel(fibres, cameras, gain, mask, own, swapped, *rest):
    *blocks_in, calibrated, model = rest
    totals = tree([part[...] for part in blocks_in[:cameras][::-1]])
    across = blocks_in[cameras:][::-1]
    me = lax.axis_index("patch")
    sky = totals[0:1, :] / (PRIOR + totals[1:2, :])
    model[...] = sky
    last = len(across)
    blocks = {0: own[0, :fibres, :], 1: swapped[last, :fibres, :]}
    for t, block in enumerate(across):
        blocks[2 * t + 2] = block[0, :fibres, :]
        blocks[2 * t + 3] = swapped[last - 1 - t, :fibres, :]
    for s, block in blocks.items():
        at = pl.ds(pl.multiple_of((me ^ s) * fibres, fibres), fibres)
        calibrated[at, :] = mask[at, 0:1] * (block - gain[0] * sky)


def finish(fibres, gain, mask, own, swapped, parts, across):
    width = own.shape[-1]
    near = pl.BlockSpec(memory_space=pltpu.VMEM)
    return pl.pallas_call(
        functools.partial(finish_kernel, fibres, len(parts)),
        in_specs=[pl.BlockSpec(memory_space=pltpu.SMEM)] + [near] * (3 + len(parts) + len(across)),
        out_specs=[near] * 2,
        out_shape=[
            jax.ShapeDtypeStruct((mask.shape[0], width), F32),
            jax.ShapeDtypeStruct((1, width), F32),
        ],
        compiler_params=pltpu.CompilerParams(vmem_limit_bytes=8 * 2**20),
        name="finish",
    )(gain, mask, own, swapped, *parts, *across)


def tree(terms):
    return terms[0] if len(terms) == 1 else tree(terms[0::2]) + tree(terms[1::2])


def swap(values, axis, shift):
    return lax.ppermute(values, axis, [(i, i ^ shift) for i in range(lax.axis_size(axis))])


def per_device(
    pixel_counts,
    pixel_weights,
    wave_profile,
    cross_profile,
    trace_columns,
    throughput,
    sky_fibres,
    fibre_mask,
):
    fibres = trace_columns.shape[1]
    parts = lax.axis_size("patch")
    cameras = lax.axis_size("ccd")
    width = pixel_counts.shape[2] // parts
    me = lax.axis_index("patch")
    columns = pixel_counts.shape[1]
    wave = wave_profile[0, 0]
    counts, weights = pixel_counts[0], pixel_weights[0]
    first = jnp.concatenate([counts[:HALO], weights[:HALO]], axis=0)
    final = jnp.concatenate([counts[columns - HALO :], weights[columns - HALO :]], axis=0)
    odd = me % 2 == 1
    outer = jnp.where(odd, final, first)
    inner = jnp.where(odd, first, final)
    far = [(i, i + 1) for i in range(1, parts - 1, 2)]
    outer = lax.ppermute(outer, "patch", far + [(b, a) for a, b in far])
    inner = swap(inner, "patch", 1)
    pixels = jnp.pad(
        jnp.concatenate([pixel_counts[0], pixel_weights[0]], axis=0), ((0, 0), (LANES, LANES))
    )
    state = prepare(trace_columns[0], cross_profile[0], pixels, wave)
    state = [*state, wave, sky_fibres, fibre_mask]
    away = relax([(s, s + 1) for s in range(2, parts, 2)], width, (), outer, inner, *state)
    across = [swap(block, "patch", 2 * t + 2) for t, block in enumerate(away)]
    state[0], *away = lax.optimization_barrier((state[0], *away))
    own, mate, mask = relax([(0,), (1,)], width, (fibre_mask.shape[1],), outer, inner, *state)
    sky = slice(fibres, fibres + 2)
    part, other = own[0, sky], mate[0, sky]
    for block in across[::-1]:
        part, other = part + block[0, sky], other + block[1, sky]
    other = swap(other, "patch", 1)
    swapped = swap(jnp.concatenate([block[1:] for block in across[::-1]] + [mate], axis=0), "patch", 1)
    part = part + other
    part = part * jnp.stack([throughput, throughput * throughput])
    sums = [part] + [swap(part, "ccd", s) for s in range(1, cameras)]
    calibrated, model = finish(fibres, throughput, mask, own, swapped, sums[::-1], across[::-1])
    return calibrated[None], model[0]


def solution(mesh):
    return jax.shard_map(
        per_device,
        mesh=mesh,
        in_specs=(
            P("ccd", "patch", None),
            P("ccd", "patch", None),
            P("ccd", "patch", None, None, None),
            P("ccd", "patch", None),
            P("ccd", "patch", None),
            P("ccd"),
            P("ccd", None),
            P("ccd", None),
        ),
        out_specs=(P("ccd", None, "patch"), P("patch")),
        check_vma=False,
    )
```
